128 devices in a mesh: comp: 2 (over y_hi), gy: 4 (over y_lo, core), gx: 16 (over z, x).
Axes of the slice: x: 4, y: 4 (y_hi: 2, y_lo: 2; y = y_hi * 2 + y_lo), z: 4, core: 2. Of those that a mesh axis runs over, the one named last changes fastest.
Arguments:
- state: float32 [2, 8, 512, 2048], P('comp', None, 'gy', 'gx'), may hold values from -6 to 6
- target: float32 [2, 8, 512, 2048], P('comp', None, 'gy', 'gx'), may hold values from -2.5 to 0.5
- land_mask: int32 [2, 512, 2048], P('comp', 'gy', 'gx'), may hold values 0 or 1
- diffusivity: float32 [2, 8], replicated, may hold values from 0.03 to 0.24
- coupling: float32 [2, 8, 4], replicated, may hold values from -3 to 3
- w_in: bfloat16 [16, 256], replicated, may hold values from -1.5 to 1.5
- b_in: float32 [256], replicated, may hold values from -3 to 3
- w_mid: bfloat16 [256, 256], replicated, may hold values from -0.375 to 0.375
- b_mid: float32 [256], replicated, may hold values from -3 to 3
- w_out: bfloat16 [256, 4], replicated, may hold values from -0.375 to 0.375
- b_out: float32 [4], replicated, may hold values from -3 to 3
- remap_weight: bfloat16 [2, 4, 16, 64, 4, 128, 128], P('comp', 'gy', 'gx'), may hold values from -0.5 to 0.5
- remap_source: int32 [2, 4, 16, 64, 4], P('comp', 'gy', 'gx'), may hold values from 0 to 127
- remap_target: int32 [2, 4, 16, 64, 4], P('comp', 'gy', 'gx'), may hold values from 0 to 127
- remap_count: int32 [2, 4, 16, 64], P('comp', 'gy', 'gx'), may hold values from 0 to 4, as said below
Outputs:
- new_state: float32 [2, 8, 512, 2048], P('comp', None, 'gy', 'gx')
- state_adjoint: float32 [2, 8, 512, 2048], P('comp', None, 'gy', 'gx')
- grad_w_in: float32 [16, 256], replicated
- grad_b_in: float32 [256], replicated
- grad_w_mid: float32 [256, 256], replicated
- grad_b_mid: float32 [256], replicated
- grad_w_out: float32 [256, 4], replicated
- grad_b_out: float32 [4], replicated
The draws below stay inside these ranges and needn't reach their ends.
Inputs may be any that keep to these rules, and one draw needn't show every extreme that they name: remap_count[c, i, j, q] leading slots of the pair are in use, the rest are padding. A pair has slots in use exactly where receiving tile q lies within 2 tile rows of i and in a tile column within 2 of j (periodic), or, for a sender in the top tile row, where q lies in the top tile row within 1 column (periodic) of column 15 - j; such pairs use 1 slot or more; for each component one receiving tile has all 4 slots in use from every such sending tile.
All inputs are finite; a program needn't handle non-finite values. No bound on the sum of `land_mask` on one device may be relied on, other than what follows from the above.
Results may differ from the reference program's by a relative error of at most 0.0037.
Values may be sent and summed in bfloat16 or wider, within the bound.
A program may use at most 64 MiB of HBM per device.

```python
import math
import jax
import jax.numpy as jnp
from jax import lax

CH = 8
FIN = 16
HID = 256
FOUT = 4
TR = 128
BW = 128
SLOTS = 4
G = 64
NY = 512
NX = 2048
N_GY = 4
N_GX = 16


def draw_remap_count(key, part):
    base_key = jax.random.fold_in(key, 11)
    pick_key = jax.random.fold_in(key, 12)
    base_count = jax.random.randint(base_key, (2, N_GY, N_GX, G), 1, SLOTS + 1)
    chosen = jax.random.randint(pick_key, (2, 1, 1, 1), 0, G)
    tile_row = jnp.arange(N_GY, dtype=jnp.int32).reshape(1, N_GY, 1, 1)
    tile_col = jnp.arange(N_GX, dtype=jnp.int32).reshape(1, 1, N_GX, 1)
    column = jnp.arange(G, dtype=jnp.int32).reshape(1, 1, 1, G)
    recv_row = column // N_GX
    recv_col = column % N_GX
    col_gap = (recv_col - tile_col) % N_GX
    near_col = jnp.logical_or(col_gap <= 2, col_gap >= N_GX - 2)
    near_row = jnp.abs(recv_row - tile_row) <= N_GY // 2
    fold_gap = (recv_col - (N_GX - 1 - tile_col)) % N_GX
    near_fold = jnp.logical_or(fold_gap <= 1, fold_gap >= N_GX - 1)
    top_pair = jnp.logical_and(tile_row == N_GY - 1, recv_row == N_GY - 1)
    live = jnp.logical_or(jnp.logical_and(near_row, near_col), jnp.logical_and(top_pair, near_fold))
    filled = jnp.where(column == chosen, SLOTS, base_count)
    return jnp.where(live, filled, 0).astype(jnp.int32)


def set_ends(drawn, key, low, top_value):
    index_at = [jax.random.randint(jax.random.fold_in(key, axis), (), 0, length) for axis, length in enumerate(drawn.shape)]
    longest = drawn.shape.index(max(drawn.shape))
    next_to = index_at[:longest] + [(index_at[longest] + 1) % drawn.shape[longest]] + index_at[longest + 1:]
    return drawn.at[tuple(index_at)].set(low).at[tuple(next_to)].set(top_value)


def block_scale(rng, extent, shards, least, largest):
    factor_of = 1.0
    for dim, shards_of in shards:
        heights = jax.random.uniform(jax.random.fold_in(jax.random.fold_in(rng, 6), dim), (shards_of,), jnp.float32, least / len(shards), largest / len(shards))
        factor_of = factor_of * jnp.repeat(jnp.exp(heights), extent[dim] // shards_of).reshape((-1,) + (1,) * (len(extent) - 1 - dim))
    return factor_of


def scatter_about(stream_key, extent, width, limit, split=(), kind=jnp.bfloat16):
    gain = block_scale(stream_key, extent, split, -0.22, 0.18) if split else 1.0
    entries = jax.random.normal(stream_key, extent, jnp.float32) * width * gain
    return jnp.minimum(jnp.maximum(entries, -limit), limit).astype(kind)


def setup_inputs(seed: int = 0) -> dict:
    arg_keys = jax.random.split(jax.random.key(seed), 16)
    return {
        "state": scatter_about(arg_keys[0], (2, CH, NY, NX), 1.0, 6.0, ((0, 2), (2, 4), (3, 16)), jnp.float32),
        "target": jnp.clip(-2.5 + 3.0 * jax.random.uniform(arg_keys[1], (2, CH, NY, NX), jnp.float32) ** block_scale(arg_keys[1], (2, CH, NY, NX), ((0, 2), (2, 4), (3, 16)), -0.2, 0.2), -2.5, 0.5),
        "land_mask": set_ends((jax.random.randint(arg_keys[2], (2, NY, NX), 0, 10) < 7).astype(jnp.int32), jax.random.fold_in(arg_keys[2], 1), 0, 1),
        "diffusivity": jnp.clip(jnp.exp(jax.random.uniform(arg_keys[3], (2, CH), jnp.float32, math.log(0.03), math.log(0.24))), 0.03, 0.24),
        "coupling": scatter_about(arg_keys[4], (2, CH, FOUT), 0.5, 3.0, (), jnp.float32),
        "w_in": scatter_about(arg_keys[5], (FIN, HID), FIN ** -0.5, 1.5),
        "b_in": scatter_about(arg_keys[6], (HID,), 0.5, 3.0, (), jnp.float32),
        "w_mid": scatter_about(arg_keys[7], (HID, HID), HID ** -0.5, 0.375),
        "b_mid": scatter_about(arg_keys[8], (HID,), 0.5, 3.0, (), jnp.float32),
        "w_out": scatter_about(arg_keys[9], (HID, FOUT), HID ** -0.5, 0.375),
        "b_out": scatter_about(arg_keys[10], (FOUT,), 0.5, 3.0, (), jnp.float32),
        "remap_weight": scatter_about(arg_keys[11], (2, N_GY, N_GX, G, SLOTS, BW, BW), BW ** -0.5, 0.5, ((0, 2), (1, 4), (2, 16))),
        "remap_source": set_ends(jax.random.randint(arg_keys[12], (2, N_GY, N_GX, G, SLOTS), 0, TR), jax.random.fold_in(arg_keys[12], 1), 0, TR - 1).astype(jnp.int32),
        "remap_target": set_ends(jax.random.randint(arg_keys[13], (2, N_GY, N_GX, G, SLOTS), 0, TR), jax.random.fold_in(arg_keys[13], 1), 0, TR - 1).astype(jnp.int32),
        "remap_count": draw_remap_count(jax.random.fold_in(arg_keys[15], 71), 0),
    }


PRECISE = lax.Precision.HIGHEST


def silu_slope(preact):
    sigmoid_value = jax.nn.sigmoid(preact)
    return sigmoid_value * (1.0 + preact * (1.0 - sigmoid_value))


def laplace(surface, folded):
    east_side = jnp.roll(surface, -1, axis=2)
    west_side = jnp.roll(surface, 1, axis=2)
    zero_row = jnp.zeros_like(surface[:, :1, :])
    south_side = jnp.concatenate([zero_row, surface[:, :-1, :]], axis=1)
    top_row = surface[:, -1:, ::-1] if folded else zero_row
    north_side = jnp.concatenate([surface[:, 1:, :], top_row], axis=1)
    return east_side + west_side + south_side + north_side - 4.0 * surface


def to_tiles(surface):
    shaped = surface.reshape(CH, N_GY, TR, N_GX, BW)
    return shaped.transpose(1, 3, 2, 0, 4).reshape(G, TR, CH, BW)


def from_tiles(tile_stack):
    shaped = tile_stack.reshape(N_GY, N_GX, TR, CH, BW)
    return shaped.transpose(3, 0, 2, 1, 4).reshape(CH, NY, NX)


def live_slots(count_row):
    slot_index = jnp.arange(SLOTS, dtype=jnp.int32)
    return (slot_index[None, :] < count_row[:, None]).astype(jnp.float32)


def remap_forward(tile_stack, weights, sources, targets, counts):
    dest_index = jnp.broadcast_to(jnp.arange(G, dtype=jnp.int32)[:, None], (G, SLOTS))

    def advance(summed, scan_item):
        sender_tile, weight, source, target_rows, count_row = scan_item
        picked = sender_tile[source].astype(jnp.float32)
        products = jnp.einsum("gsci,gsij->gscj", picked, weight.astype(jnp.float32))
        products = products * live_slots(count_row)[:, :, None, None]
        return summed.at[dest_index, target_rows].add(products), None

    initial = jnp.zeros((G, TR, CH, BW), jnp.float32)
    summed, _ = lax.scan(advance, initial, (tile_stack, weights, sources, targets, counts))
    return summed


def remap_adjoint(cot_tiles, weights, sources, targets, counts):
    dest_index = jnp.broadcast_to(jnp.arange(G, dtype=jnp.int32)[:, None], (G, SLOTS))

    def advance(unused, scan_item):
        weight, source, target_rows, count_row = scan_item
        live_mask = live_slots(count_row)[:, :, None, None]
        picked = cot_tiles[dest_index, target_rows] * live_mask
        picked = lax.optimization_barrier(picked.astype(jnp.bfloat16)).astype(jnp.float32)
        spread = jnp.einsum("gscj,gsij->gsci", picked, weight.astype(jnp.float32))
        landed = jnp.zeros((TR, CH, BW), jnp.float32).at[source].add(spread)
        return unused, landed

    _, stacked = lax.scan(advance, jnp.zeros((), jnp.float32), (weights, sources, targets, counts))
    return stacked


def grid_pass(features, surface, laplacian, goal, wet_mask, diff_mask, diffuse_rate, couple,
              w_in, b_in, w_mid, b_mid, w_out, b_out):
    cell_total = NY * NX
    block_size = math.gcd(cell_total, 8192)
    block_count = cell_total // block_size

    def to_blocks(array):
        return array.reshape(array.shape[0], block_count, block_size).transpose(1, 0, 2)

    def advance(gradients, scan_item):
        feature_block, current, lap_block, goal_block, wet_block, diff_block = scan_item
        pre_first = jnp.dot(w_in.T, feature_block, preferred_element_type=jnp.float32) + b_in[:, None]
        hidden_first = jax.nn.silu(pre_first).astype(jnp.bfloat16)
        pre_second = jnp.dot(w_mid.T, hidden_first, preferred_element_type=jnp.float32) + b_mid[:, None]
        hidden_second = jax.nn.silu(pre_second).astype(jnp.bfloat16)
        fluxes = (jnp.dot(w_out.T, hidden_second, preferred_element_type=jnp.float32) + b_out[:, None]) * wet_block
        updated = current + diffuse_rate[:, None] * diff_block * lap_block + jnp.dot(couple, fluxes, precision=PRECISE)
        misfit = updated - goal_block
        flux_cot = (wet_block * jnp.dot(couple.T, misfit, precision=PRECISE)).astype(jnp.bfloat16)
        second_cot = (jnp.dot(w_out, flux_cot, preferred_element_type=jnp.float32) * silu_slope(pre_second)).astype(jnp.bfloat16)
        first_cot = (jnp.dot(w_mid, second_cot, preferred_element_type=jnp.float32) * silu_slope(pre_first)).astype(jnp.bfloat16)
        feature_cot = jnp.dot(w_in, first_cot, preferred_element_type=jnp.float32)
        additions = (
            jnp.dot(feature_block, first_cot.T, preferred_element_type=jnp.float32),
            jnp.sum(first_cot.astype(jnp.float32), axis=1),
            jnp.dot(hidden_first, second_cot.T, preferred_element_type=jnp.float32),
            jnp.sum(second_cot.astype(jnp.float32), axis=1),
            jnp.dot(hidden_second, flux_cot.T, preferred_element_type=jnp.float32),
            jnp.sum(flux_cot.astype(jnp.float32), axis=1),
        )
        return jax.tree.map(jnp.add, gradients, additions), (updated, misfit, feature_cot)

    initial = (jnp.zeros((FIN, HID), jnp.float32), jnp.zeros((HID,), jnp.float32),
               jnp.zeros((HID, HID), jnp.float32), jnp.zeros((HID,), jnp.float32),
               jnp.zeros((HID, FOUT), jnp.float32), jnp.zeros((FOUT,), jnp.float32))
    items = (to_blocks(features), to_blocks(surface), to_blocks(laplacian), to_blocks(goal),
             to_blocks(wet_mask), to_blocks(diff_mask))
    gradients, outputs = lax.scan(advance, initial, items)

    def from_blocks(array):
        return array.transpose(1, 0, 2).reshape(array.shape[1], cell_total)

    return gradients, from_blocks(outputs[0]), from_blocks(outputs[1]), from_blocks(outputs[2])


def reference(state, target, land_mask, diffusivity, coupling, w_in, b_in, w_mid, b_mid, w_out, b_out,
              remap_weight, remap_source, remap_target, remap_count):
    rounded = lax.optimization_barrier(state.astype(jnp.bfloat16))
    weights = remap_weight.reshape(2, G, G, SLOTS, BW, BW)
    sources = remap_source.reshape(2, G, G, SLOTS)
    arrivals = remap_target.reshape(2, G, G, SLOTS)
    counts = remap_count.reshape(2, G, G)
    cell_total = NY * NX
    gradients = (jnp.zeros((FIN, HID), jnp.float32), jnp.zeros((HID,), jnp.float32),
                 jnp.zeros((HID, HID), jnp.float32), jnp.zeros((HID,), jnp.float32),
                 jnp.zeros((HID, FOUT), jnp.float32), jnp.zeros((FOUT,), jnp.float32))
    new_fields = []
    adjoints = []
    other_cots = []
    for component in range(2):
        sender = 1 - component
        targets = arrivals[component].transpose(1, 0, 2)
        summed = remap_forward(to_tiles(rounded[sender]), weights[sender], sources[sender], targets, counts[sender])
        other_fields = from_tiles(summed).astype(jnp.bfloat16).reshape(CH, cell_total)
        own_fields = rounded[component].reshape(CH, cell_total)
        if component == 0:
            features = jnp.concatenate([own_fields, other_fields], axis=0)
        else:
            features = jnp.concatenate([other_fields, own_fields], axis=0)
        wet_mask = land_mask[component].astype(jnp.float32).reshape(1, cell_total)
        diff_mask = wet_mask if component == 1 else jnp.ones_like(wet_mask)
        laplacian = laplace(state[component], component == 1).reshape(CH, cell_total)
        part_grads, updated, misfit, feature_cot = grid_pass(
            features, state[component].reshape(CH, cell_total), laplacian,
            target[component].reshape(CH, cell_total), wet_mask, diff_mask,
            diffusivity[component], coupling[component], w_in, b_in, w_mid, b_mid, w_out, b_out)
        gradients = jax.tree.map(jnp.add, gradients, part_grads)
        back_lap = laplace((diff_mask * misfit).reshape(CH, NY, NX), component == 1)
        if component == 0:
            own_cot = feature_cot[:CH]
            other_cot = feature_cot[CH:]
        else:
            own_cot = feature_cot[CH:]
            other_cot = feature_cot[:CH]
        adjoint_field = (misfit.reshape(CH, NY, NX) + diffusivity[component][:, None, None] * back_lap
                         + own_cot.reshape(CH, NY, NX))
        new_fields.append(updated.reshape(CH, NY, NX))
        adjoints.append(adjoint_field)
        other_cots.append(other_cot.reshape(CH, NY, NX))
    for component in range(2):
        receiver = 1 - component
        targets = arrivals[receiver].transpose(1, 0, 2)
        stacked = remap_adjoint(to_tiles(other_cots[receiver]), weights[component], sources[component],
                                targets, counts[component])
        adjoints[component] = adjoints[component] + from_tiles(stacked)
    inverse = 1.0 / (NY * NX)
    return (jnp.stack(new_fields), jnp.stack(adjoints), gradients[0] * inverse, gradients[1] * inverse,
            gradients[2] * inverse, gradients[3] * inverse, gradients[4] * inverse, gradients[5] * inverse)
```

```python
import jax
import jax.numpy as jnp
from jax import lax
from jax.experimental import pallas as pl
from jax.experimental.pallas import tpu as pltpu
from jax.sharding import PartitionSpec as P

MESH = pl.DeviceIdType.MESH
F32 = jnp.float32
BF16 = jnp.bfloat16
ENTRIES = 20
SLOTS = 4
TILE = 128
CH = 8
HID = 256
CHUNK = 4
PIECE = 40
NT = (((1,), (1,)), ((), ()))


def here():
    return lax.axis_index("comp"), lax.axis_index("gy"), lax.axis_index("gx")


def entry(n, i, j):
    top = i // 3
    if n < 15:
        row = top + n // 5
        shift = n % 5 - 2
        col = (j + shift + 16) % 16
        place = (i - row // 3) * 5 + 2 - shift
        return jnp.int32(1), row, col, place
    low = 1 - (i + 3) // 4
    middle = 1 - low - top
    shift, turn = n - 17, n - 16
    col = (middle * (j + shift) + (1 - middle) * (15 - j + turn) + 32) % 16
    apart = ((col - j + 18) % 16 + 11) // 16
    valid = middle + (top * apart if n < 18 else 0)
    place = middle * (i * 5 + 2 - shift) + (1 - middle) * n
    place = place - 5 * middle
    return valid, jnp.int32(3), col, place


def halo_peers(c, i, j):
    return (
        (jnp.int32(1), (c, i, (j + 15) % 16)),
        (jnp.int32(1), (c, i, (j + 1) % 16)),
        ((i + 3) // 4, (c, (i + 3) % 4, j)),
        (1 - i // 3, (c, (i + 1) % 4, j)),
        (c * (i // 3), (c, i, 15 - j)),
    )


def signal_to(barrier, device):
    pl.semaphore_signal(barrier, inc=1, device_id=device, device_id_type=MESH)


def greet(barrier, c, i, j):
    expected = jnp.int32(0)
    for n in range(ENTRIES):
        valid, row, col, _ = entry(n, i, j)
        expected = expected + valid
        if n < 15:
            signal_to(barrier, (1 - c, row, col))
        else:
            pl.when(valid == 1)(lambda row=row, col=col: signal_to(barrier, (1 - c, row, col)))
    for valid, device in halo_peers(c, i, j):
        expected = expected + valid
        pl.when(valid == 1)(lambda device=device: signal_to(barrier, device))
    return expected


def remote(src, dst, send, recv, device):
    return pltpu.make_async_remote_copy(
        src_ref=src, dst_ref=dst, send_sem=send, recv_sem=recv, device_id=device, device_id_type=MESH
    )


def halo_copies(c, i, j, ext, cols_out, cols_in, rows_in, send, recv):
    west, east, south, north, fold = halo_peers(c, i, j)
    return (
        (west[0], remote(cols_out.at[0], cols_in.at[1], send.at[0], recv.at[1], west[1])),
        (east[0], remote(cols_out.at[1], cols_in.at[0], send.at[1], recv.at[0], east[1])),
        (south[0], remote(ext.at[1], rows_in.at[1], send.at[2], recv.at[3], south[1])),
        (north[0], remote(ext.at[TILE], rows_in.at[0], send.at[3], recv.at[2], north[1])),
        (fold[0], remote(ext.at[TILE], rows_in.at[2], send.at[4], recv.at[4], fold[1])),
    )


def start_halo(copies):
    for valid, copy in copies:
        pl.when(valid == 1)(copy.start)


def wait_halo(c, i, j, ext, cols_out, cols_in, rows_in, send, recv):
    west, east, south, north, fold = halo_peers(c, i, j)
    from_west = remote(cols_out.at[0], cols_in.at[0], send.at[0], recv.at[0], west[1])
    from_east = remote(cols_out.at[1], cols_in.at[1], send.at[1], recv.at[1], east[1])
    from_south = remote(ext.at[1], rows_in.at[0], send.at[2], recv.at[2], south[1])
    from_north = remote(ext.at[TILE], rows_in.at[1], send.at[3], recv.at[3], north[1])
    from_fold = remote(ext.at[TILE], rows_in.at[2], send.at[4], recv.at[4], fold[1])
    from_west.wait_recv()
    from_east.wait_recv()

    @pl.when(south[0] == 1)
    def _():
        from_south.wait_recv()
        ext[0] = rows_in[0]

    @pl.when(north[0] == 1)
    def _():
        from_north.wait_recv()
        ext[TILE + 1] = rows_in[1]

    @pl.when(south[0] == 0)
    def _():
        ext[0] = jnp.zeros((CH, TILE), F32)

    @pl.when((north[0] == 0) & (fold[0] == 0))
    def _():
        ext[TILE + 1] = jnp.zeros((CH, TILE), F32)

    @pl.when(fold[0] == 1)
    def _():
        from_fold.wait_recv()
        down = lax.broadcasted_iota(jnp.int32, (TILE, TILE), 0)
        across = lax.broadcasted_iota(jnp.int32, (TILE, TILE), 1)
        turn = (down + across == TILE - 1).astype(F32)
        ext[TILE + 1] = jnp.dot(
            rows_in[2], turn, precision=lax.Precision.HIGHEST, preferred_element_type=F32
        )


def wait_halo_sent(c, i, j, ext, cols_out, cols_in, rows_in, send, recv):
    for valid, copy in halo_copies(c, i, j, ext, cols_out, cols_in, rows_in, send, recv):
        pl.when(valid == 1)(copy.wait_send)


def lanes():
    return lax.broadcasted_iota(jnp.int32, (CH, TILE), 1)


def edge_columns(ext, cols_out):
    lane = lanes()

    def step(group, carry):
        first, last = carry
        for k in range(8):
            row = group * 8 + k
            cells = ext[row + 1]
            first = jnp.where(lane == row, pltpu.roll(cells, row, 1), first)
            last = jnp.where(lane == row, pltpu.roll(cells, row + 1, 1), last)
        return first, last

    zero = jnp.zeros((CH, TILE), F32)
    first, last = lax.fori_loop(0, TILE // 8, step, (zero, zero))
    cols_out[0] = first
    cols_out[1] = last


def laplace_row(ext, cols_in, row, lane):
    cells = ext[row + 1]
    west = pltpu.roll(jnp.where(lane == TILE - 1, pltpu.roll(cols_in[0], TILE - 1 - row, 1), cells), 1, 1)
    east = pltpu.roll(jnp.where(lane == 0, pltpu.roll(cols_in[1], TILE - row, 1), cells), TILE - 1, 1)
    return east + west + ext[row] + ext[row + 2] - 4.0 * cells


def send_body(state, weights, source, count, ext, cols_in, landed,
              kernels, outgoing, cols_out, rows_in, load_sem, send_sem, recv_sem, hsend_sem, hrecv_sem):
    c, i, j = here()
    barrier = pltpu.get_barrier_semaphore()
    expected = greet(barrier, c, i, j)
    peers = [entry(n, i, j) for n in range(ENTRIES)]
    loads = []
    for n, (_, row, col, _) in enumerate(peers):
        load = pltpu.make_async_copy(weights.at[row * 16 + col], kernels.at[n], load_sem.at[n])
        load.start()
        loads.append(load)

    def turn(group, carry):
        for k in range(8):
            row = group * 8 + k
            ext[row + 1] = state[pl.ds(row, CH, stride=TILE), :]
        return carry

    lax.fori_loop(0, TILE // 8, turn, 0)
    edge_columns(ext, cols_out)
    pl.semaphore_wait(barrier, expected)
    halo = (c, i, j, ext, cols_out, cols_in, rows_in, hsend_sem, hrecv_sem)
    start_halo(halo_copies(*halo))
    sends = []
    for n, (valid, row, col, place) in enumerate(peers):
        sends.append(
            remote(outgoing.at[n], landed.at[place], send_sem.at[n], recv_sem.at[place], (1 - c, row, col))
        )
    for group in range(4):
        members = range(group * 5, group * 5 + 5)
        for n in members:
            loads[n].wait()
        for n in members:
            _, row, col, _ = peers[n]
            tile = row * 16 + col
            live = count[0, tile]
            parts = []
            for s in range(SLOTS):
                keep = (live > s).astype(F32)
                cells = (ext[source[tile, s] + 1] * keep).astype(BF16)
                parts.append(jnp.dot(cells, kernels[n, s], preferred_element_type=F32))
            outgoing[n] = jnp.concatenate(parts, axis=0).astype(BF16)
        for n in members:
            if n < 15:
                sends[n].start()
            else:
                pl.when(peers[n][0] == 1)(sends[n].start)
    wait_halo(*halo)
    for n, (valid, row, col, _) in enumerate(peers):
        arrival = remote(outgoing.at[n], landed.at[n], send_sem.at[n], recv_sem.at[n], (1 - c, row, col))
        if n < 15:
            arrival.wait_recv()
        else:
            pl.when(valid == 1)(arrival.wait_recv)

            @pl.when(valid == 0)
            def _(n=n):
                landed[n] = jnp.zeros((SLOTS * CH, TILE), BF16)

    for n, (valid, _, _, _) in enumerate(peers):
        if n < 15:
            sends[n].wait_send()
        else:
            pl.when(valid == 1)(sends[n].wait_send)
    wait_halo_sent(*halo)


def network_body(ext, cols_in, landed, target, land, rows_to, rate, couple, bias_out,
                 w_in, b_in, w_mid, b_mid, w_out, w_out_turned,
                 new_state, dm, base, going, grads,
                 remapped, other_cot, first_w, first_back, mid_turned, mid_half, out_half, mid_bias, hidden_ext, g_first, g_mid, g_out, g_bias):
    c, i, j = here()
    lane = lanes()
    peers = [entry(n, i, j) for n in range(ENTRIES)]
    remapped[...] = jnp.zeros_like(remapped)
    for n, (_, row, col, _) in enumerate(peers):
        tile = row * 16 + col
        block = landed[n].astype(F32)
        for s in range(SLOTS):
            to = rows_to[tile, s]
            remapped[to] = remapped[to] + block[s * CH:(s + 1) * CH]

    flip = c == 1
    given = w_in[...].astype(F32)
    own_w = jnp.where(flip, given[CH:], given[:CH])
    other_w = jnp.where(flip, given[:CH], given[CH:])
    bias = b_in[...]
    high = bias.astype(BF16).astype(F32)
    middle = (bias - high).astype(BF16).astype(F32)
    lower = bias - high - middle
    rows = lax.broadcasted_iota(jnp.int32, (16, HID), 0)
    extra = jnp.where(rows == 0, high, jnp.where(rows == 1, middle, jnp.where(rows == 2, lower, 0.0)))
    first_back[...] = jnp.concatenate([own_w, other_w], axis=0).astype(BF16)
    whole = jnp.concatenate([own_w, other_w, extra, jnp.zeros((TILE - 32, HID), F32)], axis=0)
    first_w[...] = (0.5 * whole.T).astype(BF16)
    mid = w_mid[...].astype(F32) * 0.5
    mid_half[...] = mid.astype(BF16)
    mid_turned[...] = mid.T.astype(BF16)
    out_half[...] = (w_out[...].astype(F32) * 0.5).astype(BF16)
    mid_bias[...] = jnp.broadcast_to(0.5 * b_mid[...], (TILE, HID)).T
    cells_count = CHUNK * TILE
    ones = (lax.broadcasted_iota(jnp.int32, (16, cells_count), 0) < 3).astype(BF16)
    hidden_ext[HID:, :] = ones
    g_first[...] = jnp.zeros_like(g_first)
    g_mid[...] = jnp.zeros_like(g_mid)
    g_out[...] = jnp.zeros_like(g_out)
    g_bias[...] = jnp.zeros_like(g_bias)
    sub = lax.broadcasted_iota(jnp.int32, (CH, TILE), 0)

    def column(scalars):
        out = jnp.zeros((CH, TILE), F32)
        for k, value in enumerate(scalars):
            out = jnp.where(sub == k, value, out)
        return out

    rates = column([rate[c, k] for k in range(CH)])
    pulls = [column([couple[c * CH + k, f] for k in range(CH)]) for f in range(4)]
    out_bias = column([bias_out[0, f] for f in range(4)])

    def step(index, carry):
        start = index * CHUNK
        blocks = []
        for k in range(CHUNK):
            blocks.append(
                jnp.concatenate([ext[start + k + 1], remapped[start + k]], axis=0).astype(BF16)
            )
        features = jnp.concatenate([jnp.concatenate(blocks, axis=1), ones], axis=0)
        half_first = jnp.dot(first_w[:, :32], features, preferred_element_type=F32)
        tan_first = jnp.tanh(half_first)
        up_first = 1.0 + tan_first
        act_first = half_first * up_first
        slope_first = up_first + act_first * (1.0 - tan_first)
        hidden_ext[:HID, :] = act_first.astype(BF16)
        half_second = jnp.dot(mid_turned[...], hidden_ext[:HID, :], preferred_element_type=F32)
        half_second = half_second + jnp.concatenate([mid_bias[...]] * CHUNK, axis=1)
        tan_second = jnp.tanh(half_second)
        up_second = 1.0 + tan_second
        act_second = half_second * up_second
        slope_second = up_second + act_second * (1.0 - tan_second)
        hidden_second = act_second.astype(BF16)
        raw = jnp.dot(w_out_turned[...], hidden_second, preferred_element_type=F32)
        misfits, cots = [], []
        for k in range(CHUNK):
            row = start + k
            wet = jnp.broadcast_to(land[pl.ds(row, 1), :].astype(F32), (CH, TILE))
            open_sea = jnp.where(flip, wet, 1.0)
            fluxes = (raw[:CH, k * TILE:(k + 1) * TILE] + out_bias) * wet
            updated = ext[row + 1] + rates * open_sea * laplace_row(ext, cols_in, row, lane)
            for f in range(4):
                updated = updated + pulls[f] * fluxes[f:f + 1]
            new_state[pl.ds(row, CH, stride=TILE), :] = updated
            misfit = updated - target[pl.ds(row, CH, stride=TILE), :]
            misfits.append(misfit)
            dm[row + 1] = misfit * open_sea
            cot = jnp.zeros((CH, TILE), F32)
            for f in range(4):
                cot = jnp.where(sub == f, jnp.sum(pulls[f] * misfit, axis=0, keepdims=True), cot)
            cot = jnp.concatenate([cot * wet, jnp.zeros((CH, TILE), F32)], axis=0).astype(BF16)
            cots.append(cot)
            g_bias[...] += cot.astype(F32)[:CH]
        flux_cot = jnp.concatenate(cots, axis=1)
        second_cot = (jnp.dot(out_half[...], flux_cot, preferred_element_type=F32) * slope_second).astype(BF16)
        first_cot = (jnp.dot(mid_half[...], second_cot, preferred_element_type=F32) * slope_first).astype(BF16)
        feature_cot = jnp.dot(first_back[...], first_cot, preferred_element_type=F32)
        g_first[...] += lax.dot_general(features, first_cot, NT, preferred_element_type=F32)
        g_mid[...] += lax.dot_general(hidden_ext[...], second_cot, NT, preferred_element_type=F32)
        g_out[...] += lax.dot_general(flux_cot, hidden_second, NT, preferred_element_type=F32)
        for k in range(CHUNK):
            piece = feature_cot[:, k * TILE:(k + 1) * TILE]
            base[start + k] = misfits[k] + piece[:CH]
            other_cot[start + k] = piece[CH:]
        return carry

    lax.fori_loop(0, TILE // CHUNK, step, 0)
    zero = jnp.zeros((CH, TILE), F32)
    dm[0] = zero
    dm[TILE + 1] = zero
    for n, (_, row, col, _) in enumerate(peers):
        tile = row * 16 + col
        going[n] = jnp.concatenate(
            [other_cot[rows_to[tile, s]] for s in range(SLOTS)], axis=0
        ).astype(BF16)
    grads[0:256] = g_mid[:HID, :TILE]
    grads[256:512] = g_mid[:HID, TILE:]
    for side in range(2):
        columns = slice(side * TILE, (side + 1) * TILE)
        at = 512 + side * 16
        grads[at:at + 8] = jnp.where(flip, g_first[8:16, columns], g_first[0:8, columns])
        grads[at + 8:at + 16] = jnp.where(flip, g_first[0:8, columns], g_first[8:16, columns])
        grads[544 + side * 8:552 + side * 8] = g_first[16:24, columns]
        grads[560 + side * 8:568 + side * 8] = g_mid[HID:HID + 8, columns]
        grads[576 + side * 8:584 + side * 8] = g_out[:CH, columns]
    grads[592:600] = g_bias[...]
    grads[600:640] = jnp.zeros((40, TILE), F32)


def return_body(going, dm_in, base, grads, weights, source, count, rate,
                adjoint, o_w_in, o_b_in, o_w_mid, o_b_mid, o_w_out, o_b_out,
                dm, kernels, back_in, cols_out, cols_in, rows_in, spread, anchor, first_in, mid_sum, second_in, total, whole,
                load_sem, send_sem, recv_sem, hsend_sem, hrecv_sem, s1, r1, s2, r2, s3, r3):
    c, i, j = here()
    lane = lanes()
    barrier = pltpu.get_barrier_semaphore()
    expected = greet(barrier, c, i, j) + 22
    me = c * 4 + i
    across = [(j + d) % 16 for d in range(1, 16)]
    along = [((me + d) % 8 // 4, (me + d) % 4) for d in range(1, 8)]
    for col in across:
        signal_to(barrier, (c, i, col))
    for other in along:
        signal_to(barrier, (*other, j))
    peers = [entry(n, i, j) for n in range(ENTRIES)]
    loads = []
    for n, (_, row, col, _) in enumerate(peers):
        load = pltpu.make_async_copy(weights.at[row * 16 + col], kernels.at[n], load_sem.at[n])
        load.start()
        loads.append(load)
    dm[...] = dm_in[...]
    edge_columns(dm, cols_out)
    pl.semaphore_wait(barrier, expected)
    halo = (c, i, j, dm, cols_out, cols_in, rows_in, hsend_sem, hrecv_sem)
    phase1 = [
        remote(grads.at[col], first_in.at[d], s1.at[d], r1.at[d], (c, i, col)) for d, col in enumerate(across)
    ]
    for copy in phase1:
        copy.start()
    start_halo(halo_copies(*halo))
    sends = []
    for n, (valid, row, col, place) in enumerate(peers):
        copy = remote(going.at[n], back_in.at[place], send_sem.at[n], recv_sem.at[place], (1 - c, row, col))
        sends.append(copy)
        if n < 15:
            copy.start()
        else:
            pl.when(valid == 1)(copy.start)

    for n, (_, row, col, _) in enumerate(peers):
        tile = row * 16 + col
        live = count[0, tile]
        used = peers[n][0]
        for s in range(SLOTS):
            at = source[tile, s]
            keep = (live > s).astype(F32) * used.astype(F32)
            anchor[pl.ds(n * SLOTS + s, 1), :] = (lane[:1] == at).astype(F32) * keep
    anchor[80:, :] = jnp.zeros((TILE - 80, TILE), F32)
    turned = anchor[...].T[:, :80].astype(BF16)
    both = jnp.concatenate([turned, turned], axis=1)

    for copy in phase1:
        copy.wait_recv()
    partial = grads[j]
    for d in range(15):
        partial = partial + first_in[d]
    mid_sum[...] = partial
    phase2 = [
        remote(mid_sum, second_in.at[d], s2.at[d], r2.at[d], (*other, j)) for d, other in enumerate(along)
    ]
    for copy in phase2:
        copy.start()

    wait_halo(*halo)
    sub = lax.broadcasted_iota(jnp.int32, (CH, TILE), 0)
    rates = jnp.zeros((CH, TILE), F32)
    for k in range(CH):
        rates = jnp.where(sub == k, rate[c, k], rates)

    def step(group, carry):
        for k in range(8):
            row = group * 8 + k
            adjoint[pl.ds(row, CH, stride=TILE), :] = base[row] + rates * laplace_row(dm, cols_in, row, lane)
        return carry

    lax.fori_loop(0, TILE // 8, step, 0)

    for copy in phase2:
        copy.wait_recv()
    partial = mid_sum[...]
    for d in range(7):
        partial = partial + second_in[d]
    total[...] = partial
    whole[j] = partial
    phase3 = [
        remote(total, whole.at[j], s3.at[d], r3.at[d], (c, i, col)) for d, col in enumerate(across)
    ]
    for copy in phase3:
        copy.start()

    for n, (valid, row, col, _) in enumerate(peers):
        arrival = remote(going.at[n], back_in.at[n], send_sem.at[n], recv_sem.at[n], (1 - c, row, col))
        if n < 15:
            arrival.wait_recv()
        else:
            pl.when(valid == 1)(arrival.wait_recv)

            @pl.when(valid == 0)
            def _(n=n):
                back_in[n] = jnp.zeros((SLOTS * CH, TILE), BF16)

    for n in range(ENTRIES):
        loads[n].wait()
    for n in range(ENTRIES):
        made = lax.dot_general(
            back_in[n], kernels[n].reshape(SLOTS * TILE, TILE), NT, preferred_element_type=F32
        )
        for s in range(SLOTS):
            spread[pl.ds(n * SLOTS + s, CH, stride=80), :] = made[s * CH:(s + 1) * CH, s * TILE:(s + 1) * TILE]
    for ch in range(CH):
        cells = spread[ch * 80:(ch + 1) * 80, :]
        high = cells.astype(BF16)
        low = (cells - high.astype(F32)).astype(BF16)
        adjoint[ch * TILE:(ch + 1) * TILE, :] += jnp.dot(
            both, jnp.concatenate([high, low], axis=0), preferred_element_type=F32
        )

    for d in range(15):
        remote(total, whole.at[(j + 15 - d) % 16], s3.at[d], r3.at[d], (c, i, across[d])).wait_recv()
    flat = whole[...].reshape(16 * PIECE, TILE) * (1.0 / 1048576.0)
    for side in range(2):
        columns = slice(side * TILE, (side + 1) * TILE)
        o_w_mid[:, columns] = flat[side * HID:(side + 1) * HID]
        o_w_in[:, columns] = flat[512 + side * 16:528 + side * 16]
        o_b_in[:, columns] = flat[544 + side * 8:545 + side * 8]
        o_b_mid[:, columns] = flat[560 + side * 8:561 + side * 8]
        o_w_out[:, columns] = flat[576 + side * 8:584 + side * 8]
    o_b_out[...] = jnp.broadcast_to(jnp.sum(flat[592:600], axis=1, keepdims=True), (CH, TILE))
    for n, (valid, _, _, _) in enumerate(peers):
        if n < 15:
            sends[n].wait_send()
        else:
            pl.when(valid == 1)(sends[n].wait_send)
    wait_halo_sent(*halo)
    for copy in phase1 + phase2 + phase3:
        copy.wait_send()


VM = pl.BlockSpec(memory_space=pltpu.VMEM)
SM = pl.BlockSpec(memory_space=pltpu.SMEM)
ANY = pl.BlockSpec(memory_space=pl.ANY)
DMA = pltpu.SemaphoreType.DMA


def arr(shape, dtype=F32):
    return jax.ShapeDtypeStruct(shape, dtype)


def shards(state, target, land_mask, diffusivity, coupling, w_in, b_in, w_mid, b_mid, w_out, b_out,
           remap_weight, remap_source, remap_target, remap_count):
    weights = remap_weight.reshape(64, SLOTS, TILE, TILE)
    source = remap_source.reshape(64, SLOTS)
    rows_to = remap_target.reshape(64, SLOTS)
    count = remap_count.reshape(1, 64)
    cells = state.reshape(CH * TILE, TILE)
    goal = target.reshape(CH * TILE, TILE)
    land = land_mask.reshape(TILE, TILE)
    ext, cols_in, landed = pl.pallas_call(
        send_body,
        out_shape=(arr((TILE + 2, CH, TILE)), arr((2, CH, TILE)), arr((ENTRIES, SLOTS * CH, TILE), BF16)),
        in_specs=[VM, ANY, SM, SM],
        out_specs=(VM, VM, VM),
        scratch_shapes=[
            pltpu.VMEM((ENTRIES, SLOTS, TILE, TILE), BF16),
            pltpu.VMEM((ENTRIES, SLOTS * CH, TILE), BF16),
            pltpu.VMEM((2, CH, TILE), F32),
            pltpu.VMEM((3, CH, TILE), F32),
            DMA((ENTRIES,)), DMA((ENTRIES,)), DMA((ENTRIES,)), DMA((5,)), DMA((5,)),
        ],
        compiler_params=pltpu.CompilerParams(
            collective_id=0, has_side_effects=True, vmem_limit_bytes=24 << 20
        ),
        name="remap_send",
    )(cells, weights, source, count)

    new_state, dm, base, going, grads = pl.pallas_call(
        network_body,
        out_shape=(
            arr((CH * TILE, TILE)),
            arr((TILE + 2, CH, TILE)),
            arr((TILE, CH, TILE)),
            arr((ENTRIES, SLOTS * CH, TILE), BF16),
            arr((16 * PIECE, TILE)),
        ),
        in_specs=[VM] * 5 + [SM] * 4 + [VM] * 6,
        out_specs=(VM,) * 5,
        scratch_shapes=[
            pltpu.VMEM((TILE, CH, TILE), F32),
            pltpu.VMEM((TILE, CH, TILE), F32),
            pltpu.VMEM((HID, TILE), BF16),
            pltpu.VMEM((16, HID), BF16),
            pltpu.VMEM((HID, HID), BF16),
            pltpu.VMEM((HID, HID), BF16),
            pltpu.VMEM((HID, 16), BF16),
            pltpu.VMEM((HID, TILE), F32),
            pltpu.VMEM((HID + 16, CHUNK * TILE), BF16),
            pltpu.VMEM((32, HID), F32),
            pltpu.VMEM((HID + 16, HID), F32),
            pltpu.VMEM((16, HID), F32),
            pltpu.VMEM((CH, TILE), F32),
        ],
        compiler_params=pltpu.CompilerParams(vmem_limit_bytes=32 << 20),
        name="network",
    )(
        ext, cols_in, landed, goal, land, rows_to, diffusivity, coupling.reshape(2 * CH, 4), b_out.reshape(1, 4),
        w_in, b_in.reshape(1, HID), w_mid, b_mid.reshape(1, HID),
        jnp.pad(w_out, ((0, 0), (0, 12))), jnp.pad(w_out.T, ((0, 12), (0, 0))),
    )

    adjoint, g_w_in, g_b_in, g_w_mid, g_b_mid, g_w_out, g_b_out = pl.pallas_call(
        return_body,
        out_shape=(
            arr((CH * TILE, TILE)), arr((16, HID)), arr((1, HID)), arr((HID, HID)), arr((1, HID)),
            arr((CH, HID)), arr((CH, TILE)),
        ),
        in_specs=[VM] * 4 + [ANY] + [SM] * 3,
        out_specs=(VM,) * 7,
        scratch_shapes=[
            pltpu.VMEM((TILE + 2, CH, TILE), F32),
            pltpu.VMEM((ENTRIES, SLOTS, TILE, TILE), BF16),
            pltpu.VMEM((ENTRIES, SLOTS * CH, TILE), BF16),
            pltpu.VMEM((2, CH, TILE), F32),
            pltpu.VMEM((2, CH, TILE), F32),
            pltpu.VMEM((3, CH, TILE), F32),
            pltpu.VMEM((ENTRIES * SLOTS * CH, TILE), F32),
            pltpu.VMEM((TILE, TILE), F32),
            pltpu.VMEM((15, PIECE, TILE), F32),
            pltpu.VMEM((PIECE, TILE), F32),
            pltpu.VMEM((7, PIECE, TILE), F32),
            pltpu.VMEM((PIECE, TILE), F32),
            pltpu.VMEM((16, PIECE, TILE), F32),
            DMA((ENTRIES,)), DMA((ENTRIES,)), DMA((ENTRIES,)), DMA((5,)), DMA((5,)),
            DMA((15,)), DMA((15,)), DMA((7,)), DMA((7,)), DMA((15,)), DMA((15,)),
        ],
        compiler_params=pltpu.CompilerParams(
            collective_id=1, has_side_effects=True, vmem_limit_bytes=32 << 20
        ),
        name="remap_return",
    )(going, dm, base, grads.reshape(16, PIECE, TILE), weights, source, count, diffusivity)
    return (
        new_state.reshape(1, CH, TILE, TILE),
        adjoint.reshape(1, CH, TILE, TILE),
        g_w_in,
        g_b_in.reshape(HID),
        g_w_mid,
        g_b_mid.reshape(HID),
        g_w_out[:4].T,
        g_b_out[:4, 0],
    )


def solution(mesh):
    tiles = P("comp", None, "gy", "gx")
    pairs = P("comp", "gy", "gx")
    return jax.shard_map(
        shards,
        mesh=mesh,
        in_specs=(tiles, tiles, pairs) + (P(),) * 8 + (pairs,) * 4,
        out_specs=(tiles, tiles) + (P(),) * 6,
        check_vma=False,
    )
```

```python
import jax
import jax.numpy as jnp
from jax import lax
from jax.experimental import pallas as pl
from jax.experimental.pallas import tpu as pltpu
from jax.sharding import PartitionSpec as P

MESH = pl.DeviceIdType.MESH
F32 = jnp.float32
BF16 = jnp.bfloat16
ENTRIES = 20
SLOTS = 4
TILE = 128
CH = 8
HID = 256
CHUNK = 8
PIECE = 40
WIDE = 256
NT = (((1,), (1,)), ((), ()))


def here():
    return lax.axis_index("comp"), lax.axis_index("gy"), lax.axis_index("gx")


def entry(n, i, j):
    top = i // 3
    if n < 15:
        row = top + n // 5
        shift = n % 5 - 2
        col = (j + shift + 16) % 16
        place = (i - row // 3) * 5 + 2 - shift
        return jnp.int32(1), row, col, place
    low = 1 - (i + 3) // 4
    middle = 1 - low - top
    shift, turn = n - 17, n - 16
    col = (middle * (j + shift) + (1 - middle) * (15 - j + turn) + 32) % 16
    apart = ((col - j + 18) % 16 + 11) // 16
    valid = middle + (top * apart if n < 18 else 0)
    place = middle * (i * 5 + 2 - shift) + (1 - middle) * n
    place = place - 5 * middle
    return valid, jnp.int32(3), col, place


def halo_peers(c, i, j):
    return (
        (jnp.int32(1), (c, i, (j + 15) % 16)),
        (jnp.int32(1), (c, i, (j + 1) % 16)),
        ((i + 3) // 4, (c, (i + 3) % 4, j)),
        (1 - i // 3, (c, (i + 1) % 4, j)),
        (c * (i // 3), (c, i, 15 - j)),
    )


def signal_to(barrier, device):
    pl.semaphore_signal(barrier, inc=1, device_id=device, device_id_type=MESH)


def greet(barrier, c, i, j):
    expected = jnp.int32(0)
    for n in range(ENTRIES):
        valid, row, col, _ = entry(n, i, j)
        expected = expected + valid
        if n < 15:
            signal_to(barrier, (1 - c, row, col))
        else:
            pl.when(valid == 1)(lambda row=row, col=col: signal_to(barrier, (1 - c, row, col)))
    for valid, device in halo_peers(c, i, j):
        expected = expected + valid
        pl.when(valid == 1)(lambda device=device: signal_to(barrier, device))
    return expected


def remote(src, dst, send, recv, device):
    return pltpu.make_async_remote_copy(
        src_ref=src, dst_ref=dst, send_sem=send, recv_sem=recv, device_id=device, device_id_type=MESH
    )


def halo_copies(c, i, j, ext, cols_out, cols_in, rows_in, send, recv):
    west, east, south, north, fold = halo_peers(c, i, j)
    return (
        (west[0], remote(cols_out.at[0], cols_in.at[1], send.at[0], recv.at[1], west[1])),
        (east[0], remote(cols_out.at[1], cols_in.at[0], send.at[1], recv.at[0], east[1])),
        (south[0], remote(ext.at[1], rows_in.at[1], send.at[2], recv.at[3], south[1])),
        (north[0], remote(ext.at[TILE], rows_in.at[0], send.at[3], recv.at[2], north[1])),
        (fold[0], remote(ext.at[TILE], rows_in.at[2], send.at[4], recv.at[4], fold[1])),
    )


def start_halo(copies):
    for valid, copy in copies:
        pl.when(valid == 1)(copy.start)


def wait_halo(c, i, j, ext, cols_out, cols_in, rows_in, send, recv):
    west, east, south, north, fold = halo_peers(c, i, j)
    from_west = remote(cols_out.at[0], cols_in.at[0], send.at[0], recv.at[0], west[1])
    from_east = remote(cols_out.at[1], cols_in.at[1], send.at[1], recv.at[1], east[1])
    from_south = remote(ext.at[1], rows_in.at[0], send.at[2], recv.at[2], south[1])
    from_north = remote(ext.at[TILE], rows_in.at[1], send.at[3], recv.at[3], north[1])
    from_fold = remote(ext.at[TILE], rows_in.at[2], send.at[4], recv.at[4], fold[1])
    from_west.wait_recv()
    from_east.wait_recv()

    @pl.when(south[0] == 1)
    def _():
        from_south.wait_recv()
        ext[0] = rows_in[0]

    @pl.when(north[0] == 1)
    def _():
        from_north.wait_recv()
        ext[TILE + 1] = rows_in[1]

    @pl.when(south[0] == 0)
    def _():
        ext[0] = jnp.zeros((CH, TILE), F32)

    @pl.when((north[0] == 0) & (fold[0] == 0))
    def _():
        ext[TILE + 1] = jnp.zeros((CH, TILE), F32)

    @pl.when(fold[0] == 1)
    def _():
        from_fold.wait_recv()
        down = lax.broadcasted_iota(jnp.int32, (TILE, TILE), 0)
        across = lax.broadcasted_iota(jnp.int32, (TILE, TILE), 1)
        turn = (down + across == TILE - 1).astype(F32)
        ext[TILE + 1] = jnp.dot(
            rows_in[2], turn, precision=lax.Precision.HIGHEST, preferred_element_type=F32
        )


def wait_halo_sent(c, i, j, ext, cols_out, cols_in, rows_in, send, recv):
    for valid, copy in halo_copies(c, i, j, ext, cols_out, cols_in, rows_in, send, recv):
        pl.when(valid == 1)(copy.wait_send)


def lanes():
    return lax.broadcasted_iota(jnp.int32, (CH, TILE), 1)


def edge_columns(ext, cols_out):
    lane = lanes()

    def step(group, carry):
        first, last = carry
        for k in range(8):
            row = group * 8 + k
            cells = ext[row + 1]
            first = jnp.where(lane == row, pltpu.roll(cells, row, 1), first)
            last = jnp.where(lane == row, pltpu.roll(cells, row + 1, 1), last)
        return first, last

    zero = jnp.zeros((CH, TILE), F32)
    first, last = lax.fori_loop(0, TILE // 8, step, (zero, zero))
    cols_out[0] = first
    cols_out[1] = last


def laplace_row(ext, cols_in, row, lane):
    cells = ext[row + 1]
    west = pltpu.roll(jnp.where(lane == TILE - 1, pltpu.roll(cols_in[0], TILE - 1 - row, 1), cells), 1, 1)
    east = pltpu.roll(jnp.where(lane == 0, pltpu.roll(cols_in[1], TILE - row, 1), cells), TILE - 1, 1)
    return east + west + ext[row] + ext[row + 2] - 4.0 * cells


def send_body(state_in, weights, source_in, count_in, ext, cols_in, landed,
              state, source, count, kernels, outgoing, cols_out, rows_in, load_sem, send_sem, recv_sem, hsend_sem, hrecv_sem, in_sem):
    c, i, j = here()
    firsts = [
        pltpu.make_async_copy(given, held, in_sem.at[k])
        for k, (given, held) in enumerate(((state_in, state), (source_in, source), (count_in, count)))
    ]
    for load in firsts:
        load.start()
    barrier = pltpu.get_barrier_semaphore()
    expected = greet(barrier, c, i, j)
    peers = [entry(n, i, j) for n in range(ENTRIES)]
    loads = []
    for n, (_, row, col, _) in enumerate(peers):
        load = pltpu.make_async_copy(weights.at[row * 16 + col], kernels.at[n], load_sem.at[n])
        load.start()
        loads.append(load)
    for load in firsts:
        load.wait()

    def turn(group, carry):
        for k in range(8):
            row = group * 8 + k
            ext[row + 1] = state[pl.ds(row, CH, stride=TILE), :]
        return carry

    lax.fori_loop(0, TILE // 8, turn, 0)
    edge_columns(ext, cols_out)
    pl.semaphore_wait(barrier, expected)
    halo = (c, i, j, ext, cols_out, cols_in, rows_in, hsend_sem, hrecv_sem)
    start_halo(halo_copies(*halo))
    sends = []
    for n, (valid, row, col, place) in enumerate(peers):
        sends.append(
            remote(outgoing.at[n], landed.at[place], send_sem.at[n], recv_sem.at[place], (1 - c, row, col))
        )
    for group in range(4):
        members = range(group * 5, group * 5 + 5)
        for n in members:
            loads[n].wait()
        for n in members:
            _, row, col, _ = peers[n]
            tile = row * 16 + col
            live = count[0, tile]
            parts = []
            for s in range(SLOTS):
                keep = (live > s).astype(F32)
                cells = (ext[source[s, tile] + 1] * keep).astype(BF16)
                parts.append(jnp.dot(cells, kernels[n, s], preferred_element_type=F32))
            outgoing[n] = jnp.concatenate(parts, axis=0).astype(BF16)
        for n in members:
            if n < 15:
                sends[n].start()
            else:
                pl.when(peers[n][0] == 1)(sends[n].start)
    wait_halo(*halo)
    for n, (valid, row, col, _) in enumerate(peers):
        arrival = remote(outgoing.at[n], landed.at[n], send_sem.at[n], recv_sem.at[n], (1 - c, row, col))
        if n < 15:
            arrival.wait_recv()
        else:
            pl.when(valid == 1)(arrival.wait_recv)

            @pl.when(valid == 0)
            def _(n=n):
                landed[n] = jnp.zeros((SLOTS * CH, TILE), BF16)

    for n, (valid, _, _, _) in enumerate(peers):
        if n < 15:
            sends[n].wait_send()
        else:
            pl.when(valid == 1)(sends[n].wait_send)
    wait_halo_sent(*halo)


def network_body(ext, cols_in, landed, target, land, rows_to, rate, couple, bias_out,
                 w_in, b_in, w_mid, b_mid, w_out,
                 new_state, dm, base, going, grads,
                 remapped, other_cot, first_w, first_back, mid_turned, mid_half, out_half, w_out_turned, mid_bias, g_first, g_mid, g_out, g_bias, *kept):
    c, i, j = here()
    lane = lanes()
    peers = [entry(n, i, j) for n in range(ENTRIES)]
    remapped[...] = jnp.zeros_like(remapped)
    for n, (_, row, col, _) in enumerate(peers):
        tile = row * 16 + col
        block = landed[n].astype(F32)
        for s in range(SLOTS):
            to = rows_to[s, tile]
            remapped[to] = remapped[to] + block[s * CH:(s + 1) * CH]

    flip = c == 1
    given = w_in[...].astype(F32)
    own_w = jnp.where(flip, given[CH:], given[:CH])
    other_w = jnp.where(flip, given[:CH], given[CH:])
    bias = b_in[...]
    high = bias.astype(BF16).astype(F32)
    middle = (bias - high).astype(BF16).astype(F32)
    lower = bias - high - middle
    rows = lax.broadcasted_iota(jnp.int32, (16, HID), 0)
    extra = jnp.where(rows == 0, high, jnp.where(rows == 1, middle, jnp.where(rows == 2, lower, 0.0)))
    first_back[...] = jnp.concatenate([own_w, other_w], axis=0).astype(BF16)
    whole = jnp.concatenate([own_w, other_w, extra, jnp.zeros((TILE - 32, HID), F32)], axis=0)
    first_w[...] = (0.5 * whole.T).astype(BF16)
    mid = w_mid[...].astype(F32) * 0.5
    mid_half[...] = mid.astype(BF16)
    mid_turned[...] = mid.T.astype(BF16)
    tall = jnp.concatenate([w_out[...].astype(F32), jnp.zeros((TILE - 4, HID), F32)], axis=0)
    w_out_turned[...] = tall[:16].astype(BF16)
    out_half[...] = (0.5 * tall.T)[:, :16].astype(BF16)
    mid_bias[...] = jnp.broadcast_to(0.5 * b_mid[...], (TILE, HID)).T
    ones = (lax.broadcasted_iota(jnp.int32, (16, WIDE), 0) < 3).astype(BF16)
    for p in range(CHUNK * TILE // WIDE):
        kept[1][HID:, p * WIDE:(p + 1) * WIDE] = ones
        kept[10][HID:, p * WIDE:(p + 1) * WIDE] = ones
    g_first[...] = jnp.zeros_like(g_first)
    g_mid[...] = jnp.zeros_like(g_mid)
    g_out[...] = jnp.zeros_like(g_out)
    g_bias[...] = jnp.zeros_like(g_bias)
    sub = lax.broadcasted_iota(jnp.int32, (CH, TILE), 0)

    def column(scalars):
        out = jnp.zeros((CH, TILE), F32)
        for k, value in enumerate(scalars):
            out = jnp.where(sub == k, value, out)
        return out

    rates = column([rate[c, k] for k in range(CH)])
    pulls = [column([couple[c, f, k] for k in range(CH)]) for f in range(4)]
    out_bias = column([bias_out[0, f] for f in range(4)])

    def forward(start, part, features_ref, hidden_ref, slope_one, slope_two, second_ref, raw_ref, *_):
        span = slice(part * WIDE, (part + 1) * WIDE)
        first_row = start + part * (WIDE // TILE)
        blocks = [
            jnp.concatenate([ext[first_row + k + 1], remapped[first_row + k]], axis=0).astype(BF16)
            for k in range(WIDE // TILE)
        ]
        features = jnp.concatenate([jnp.concatenate(blocks, axis=1), ones], axis=0)
        features_ref[:, span] = features
        half_first = jnp.dot(first_w[:, :32], features, preferred_element_type=F32)
        yield
        tan_first = jnp.tanh(half_first)
        up_first = 1.0 + tan_first
        act_first = half_first * up_first
        slope_one[:, span] = up_first + act_first * (1.0 - tan_first)
        hidden_first = act_first.astype(BF16)
        hidden_ref[:HID, span] = hidden_first
        half_second = jnp.dot(mid_turned[...], hidden_first, preferred_element_type=F32)
        yield
        half_second = half_second + jnp.concatenate([mid_bias[...]] * (WIDE // TILE), axis=1)
        tan_second = jnp.tanh(half_second)
        up_second = 1.0 + tan_second
        act_second = half_second * up_second
        slope_two[:, span] = up_second + act_second * (1.0 - tan_second)
        hidden_second = act_second.astype(BF16)
        second_ref[:, span] = hidden_second
        raw_ref[:, span] = jnp.dot(w_out_turned[...], hidden_second, preferred_element_type=F32)
        yield

    def backward(start, part, features_ref, hidden_ref, slope_one, slope_two, second_ref, raw_ref, one_ref, two_ref, cot_ref):
        span = slice(part * WIDE, (part + 1) * WIDE)
        first_row = start + part * (WIDE // TILE)
        raw = raw_ref[:CH, span]
        misfits, cots = [], []
        for k in range(WIDE // TILE):
            row = first_row + k
            wet = jnp.broadcast_to(land[pl.ds(row, 1), :].astype(F32), (CH, TILE))
            open_sea = jnp.where(flip, wet, 1.0)
            fluxes = (raw[:, k * TILE:(k + 1) * TILE] + out_bias) * wet
            updated = ext[row + 1] + rates * open_sea * laplace_row(ext, cols_in, row, lane)
            for f in range(4):
                updated = updated + pulls[f] * fluxes[f:f + 1]
            new_state[pl.ds(row, CH, stride=TILE), :] = updated
            misfit = updated - target[pl.ds(row, CH, stride=TILE), :]
            misfits.append(misfit)
            dm[row + 1] = misfit * open_sea
            cot = jnp.zeros((CH, TILE), F32)
            for f in range(4):
                cot = jnp.where(sub == f, jnp.sum(pulls[f] * misfit, axis=0, keepdims=True), cot)
            cot = jnp.concatenate([cot * wet, jnp.zeros((CH, TILE), F32)], axis=0).astype(BF16)
            cots.append(cot)
            g_bias[...] += cot.astype(F32)[:CH]
        flux_cot = jnp.concatenate(cots, axis=1)
        cot_ref[:, span] = flux_cot
        pulled = jnp.dot(out_half[...], flux_cot, preferred_element_type=F32)
        yield
        second_cot = (pulled * slope_two[:, span]).astype(BF16)
        two_ref[:, span] = second_cot
        pulled = jnp.dot(mid_half[...], second_cot, preferred_element_type=F32)
        yield
        first_cot = (pulled * slope_one[:, span]).astype(BF16)
        one_ref[:, span] = first_cot
        feature_cot = jnp.dot(first_back[...], first_cot, preferred_element_type=F32)
        yield
        for k in range(WIDE // TILE):
            piece = feature_cot[:, k * TILE:(k + 1) * TILE]
            base[first_row + k] = misfits[k] + piece[:CH]
            other_cot[first_row + k] = piece[CH:]

    def gradients(features_ref, hidden_ref, slope_one, slope_two, second_ref, raw_ref, one_ref, two_ref, cot_ref):
        g_mid[...] += lax.dot_general(hidden_ref[...], two_ref[...], NT, preferred_element_type=F32)
        g_out[...] += lax.dot_general(cot_ref[...], second_ref[...], NT, preferred_element_type=F32)
        g_first[...] += lax.dot_general(features_ref[...], one_ref[...], NT, preferred_element_type=F32)

    def play(*chains):
        chains = list(chains)
        while chains:
            chains = [chain for chain in chains if next(chain, chain) is not chain]

    PARTS = CHUNK * TILE // WIDE
    half = len(kept) // 2
    even, odd = kept[:half], kept[half:]
    play(*(forward(0, p, *even) for p in range(PARTS)))

    def both(back_at, back, front_at, front):
        chains = []
        for p in range(PARTS):
            chains.append(forward(front_at, p, *front))
            chains.append(backward(back_at, p, *back))
        play(*chains)
        gradients(*back)

    def step(pair, carry):
        at = pair * (2 * CHUNK)
        both(at, even, at + CHUNK, odd)
        both(at + CHUNK, odd, jnp.minimum(at + 2 * CHUNK, TILE - CHUNK), even)
        return carry

    lax.fori_loop(0, TILE // (2 * CHUNK), step, 0)
    zero = jnp.zeros((CH, TILE), F32)
    dm[0] = zero
    dm[TILE + 1] = zero
    for n, (_, row, col, _) in enumerate(peers):
        tile = row * 16 + col
        going[n] = jnp.concatenate(
            [other_cot[rows_to[s, tile]] for s in range(SLOTS)], axis=0
        ).astype(BF16)
    grads[0:256] = g_mid[:HID, :TILE]
    grads[256:512] = g_mid[:HID, TILE:]
    for side in range(2):
        columns = slice(side * TILE, (side + 1) * TILE)
        at = 512 + side * 16
        grads[at:at + 8] = jnp.where(flip, g_first[8:16, columns], g_first[0:8, columns])
        grads[at + 8:at + 16] = jnp.where(flip, g_first[0:8, columns], g_first[8:16, columns])
        grads[544 + side * 8:552 + side * 8] = g_first[16:24, columns]
        grads[560 + side * 8:568 + side * 8] = g_mid[HID:HID + 8, columns]
        grads[576 + side * 8:584 + side * 8] = g_out[:CH, columns]
    grads[592:600] = g_bias[...]
    grads[600:640] = jnp.zeros((40, TILE), F32)


def return_body(going, dm_in, base, grads, weights, source, count, rate,
                adjoint, whole,
                dm, kernels, back_in, cols_out, cols_in, rows_in, spread, anchor, first_in, mid_sum, second_in, total,
                load_sem, send_sem, recv_sem, hsend_sem, hrecv_sem, s1, r1, s2, r2, s3, r3):
    c, i, j = here()
    lane = lanes()
    barrier = pltpu.get_barrier_semaphore()
    expected = greet(barrier, c, i, j) + 22
    me = c * 4 + i
    across = [(j + d) % 16 for d in range(1, 16)]
    along = [((me + d) % 8 // 4, (me + d) % 4) for d in range(1, 8)]
    for col in across:
        signal_to(barrier, (c, i, col))
    for other in along:
        signal_to(barrier, (*other, j))
    peers = [entry(n, i, j) for n in range(ENTRIES)]
    loads = []
    for n, (_, row, col, _) in enumerate(peers):
        load = pltpu.make_async_copy(weights.at[row * 16 + col], kernels.at[n], load_sem.at[n])
        load.start()
        loads.append(load)
    dm[...] = dm_in[...]
    edge_columns(dm, cols_out)
    pl.semaphore_wait(barrier, expected)
    halo = (c, i, j, dm, cols_out, cols_in, rows_in, hsend_sem, hrecv_sem)
    phase1 = [
        remote(grads.at[col], first_in.at[d], s1.at[d], r1.at[d], (c, i, col)) for d, col in enumerate(across)
    ]
    for copy in phase1:
        copy.start()
    start_halo(halo_copies(*halo))
    sends = []
    for n, (valid, row, col, place) in enumerate(peers):
        copy = remote(going.at[n], back_in.at[place], send_sem.at[n], recv_sem.at[place], (1 - c, row, col))
        sends.append(copy)
        if n < 15:
            copy.start()
        else:
            pl.when(valid == 1)(copy.start)

    for n, (_, row, col, _) in enumerate(peers):
        tile = row * 16 + col
        live = count[0, tile]
        used = peers[n][0]
        for s in range(SLOTS):
            at = source[s, tile]
            keep = (live > s).astype(F32) * used.astype(F32)
            anchor[pl.ds(n * SLOTS + s, 1), :] = (lane[:1] == at).astype(F32) * keep
    anchor[80:, :] = jnp.zeros((TILE - 80, TILE), F32)
    turned = anchor[...].T[:, :80].astype(BF16)
    both = jnp.concatenate([turned, turned], axis=1)

    for copy in phase1:
        copy.wait_recv()
    partial = grads[j]
    for d in range(15):
        partial = partial + first_in[d]
    mid_sum[...] = partial
    phase2 = [
        remote(mid_sum, second_in.at[d], s2.at[d], r2.at[d], (*other, j)) for d, other in enumerate(along)
    ]
    for copy in phase2:
        copy.start()

    wait_halo(*halo)
    sub = lax.broadcasted_iota(jnp.int32, (CH, TILE), 0)
    rates = jnp.zeros((CH, TILE), F32)
    for k in range(CH):
        rates = jnp.where(sub == k, rate[c, k], rates)

    def step(group, carry):
        for k in range(8):
            row = group * 8 + k
            adjoint[pl.ds(row, CH, stride=TILE), :] = base[row] + rates * laplace_row(dm, cols_in, row, lane)
        return carry

    lax.fori_loop(0, TILE // 8, step, 0)

    for copy in phase2:
        copy.wait_recv()
    partial = mid_sum[...]
    for d in range(7):
        partial = partial + second_in[d]
    total[...] = partial
    whole[j] = partial
    phase3 = [
        remote(total, whole.at[j], s3.at[d], r3.at[d], (c, i, col)) for d, col in enumerate(across)
    ]
    for copy in phase3:
        copy.start()

    for n, (valid, row, col, _) in enumerate(peers):
        arrival = remote(going.at[n], back_in.at[n], send_sem.at[n], recv_sem.at[n], (1 - c, row, col))
        if n < 15:
            arrival.wait_recv()
        else:
            pl.when(valid == 1)(arrival.wait_recv)

            @pl.when(valid == 0)
            def _(n=n):
                back_in[n] = jnp.zeros((SLOTS * CH, TILE), BF16)

    for n in range(ENTRIES):
        loads[n].wait()
    for n in range(ENTRIES):
        made = lax.dot_general(
            back_in[n], kernels[n].reshape(SLOTS * TILE, TILE), NT, preferred_element_type=F32
        )
        for s in range(SLOTS):
            spread[pl.ds(n * SLOTS + s, CH, stride=80), :] = made[s * CH:(s + 1) * CH, s * TILE:(s + 1) * TILE]
    for ch in range(CH):
        cells = spread[ch * 80:(ch + 1) * 80, :]
        high = cells.astype(BF16)
        low = (cells - high.astype(F32)).astype(BF16)
        adjoint[ch * TILE:(ch + 1) * TILE, :] += jnp.dot(
            both, jnp.concatenate([high, low], axis=0), preferred_element_type=F32
        )

    for d in range(15):
        remote(total, whole.at[(j + 15 - d) % 16], s3.at[d], r3.at[d], (c, i, across[d])).wait_recv()
    for n, (valid, _, _, _) in enumerate(peers):
        if n < 15:
            sends[n].wait_send()
        else:
            pl.when(valid == 1)(sends[n].wait_send)
    wait_halo_sent(*halo)
    for copy in phase1 + phase2 + phase3:
        copy.wait_send()


def finish_body(adjoint_in, whole, adjoint, o_w_in, o_b_in, o_w_mid, o_b_mid, o_w_out, o_b_out, sem):
    copy = pltpu.make_async_copy(adjoint_in, adjoint, sem)
    copy.start()
    flat = whole[...] * (1.0 / 1048576.0)
    for side in range(2):
        columns = slice(side * TILE, (side + 1) * TILE)
        o_w_mid[:, columns] = flat[side * HID:(side + 1) * HID]
        o_w_in[:, columns] = flat[512 + side * 16:528 + side * 16]
        o_b_in[:, columns] = flat[544 + side * 8:545 + side * 8]
        o_b_mid[:, columns] = flat[560 + side * 8:561 + side * 8]
        o_w_out[:, columns] = flat[576 + side * 8:580 + side * 8]
    sums = jnp.broadcast_to(jnp.sum(flat[592:600], axis=1, keepdims=True), (CH, TILE))
    sub = lax.broadcasted_iota(jnp.int32, (CH, TILE), 0)
    picked = jnp.sum(jnp.where(sub == lanes(), sums, 0.0), axis=0, keepdims=True)
    o_b_out[...] = picked[:, :4]
    copy.wait()


VM = pl.BlockSpec(memory_space=pltpu.VMEM)
SM = pl.BlockSpec(memory_space=pltpu.SMEM)
HB = pl.BlockSpec(memory_space=pltpu.HBM)
DMA = pltpu.SemaphoreType.DMA


def arr(shape, dtype=F32):
    return jax.ShapeDtypeStruct(shape, dtype)


def network_call(*args):
    return pl.pallas_call(
        network_body,
        out_shape=(
            arr((CH * TILE, TILE)),
            arr((TILE + 2, CH, TILE)),
            arr((TILE, CH, TILE)),
            arr((ENTRIES, SLOTS * CH, TILE), BF16),
            arr((16 * PIECE, TILE)),
        ),
        in_specs=[VM] * 5 + [SM] * 4 + [VM] * 5,
        out_specs=(VM,) * 5,
        scratch_shapes=[
            pltpu.VMEM((TILE, CH, TILE), F32),
            pltpu.VMEM((TILE, CH, TILE), F32),
            pltpu.VMEM((HID, TILE), BF16),
            pltpu.VMEM((16, HID), BF16),
            pltpu.VMEM((HID, HID), BF16),
            pltpu.VMEM((HID, HID), BF16),
            pltpu.VMEM((HID, 16), BF16),
            pltpu.VMEM((16, HID), BF16),
            pltpu.VMEM((HID, TILE), F32),
            pltpu.VMEM((32, HID), F32),
            pltpu.VMEM((HID + 16, HID), F32),
            pltpu.VMEM((16, HID), F32),
            pltpu.VMEM((CH, TILE), F32),
        ]
        + [
            pltpu.VMEM((32, CHUNK * TILE), BF16),
            pltpu.VMEM((HID + 16, CHUNK * TILE), BF16),
            pltpu.VMEM((HID, CHUNK * TILE), F32),
            pltpu.VMEM((HID, CHUNK * TILE), F32),
            pltpu.VMEM((HID, CHUNK * TILE), BF16),
            pltpu.VMEM((16, CHUNK * TILE), F32),
            pltpu.VMEM((HID, CHUNK * TILE), BF16),
            pltpu.VMEM((HID, CHUNK * TILE), BF16),
            pltpu.VMEM((16, CHUNK * TILE), BF16),
        ] * 2,
        compiler_params=pltpu.CompilerParams(vmem_limit_bytes=48 << 20),
        name="network",
    )(*args)


def shards(state, target, land_mask, diffusivity, coupling, w_in, b_in, w_mid, b_mid, w_out, b_out,
           remap_weight, remap_source, remap_target, remap_count):
    weights = remap_weight.reshape(64, SLOTS, TILE, TILE)
    source = remap_source.reshape(64, SLOTS).T
    rows_to = remap_target.reshape(64, SLOTS).T
    count = remap_count.reshape(1, 64)
    cells = state.reshape(CH * TILE, TILE)
    goal = target.reshape(CH * TILE, TILE)
    land = land_mask.reshape(TILE, TILE)
    ext, cols_in, landed = pl.pallas_call(
        send_body,
        out_shape=(arr((TILE + 2, CH, TILE)), arr((2, CH, TILE)), arr((ENTRIES, SLOTS * CH, TILE), BF16)),
        in_specs=[HB] * 4,
        out_specs=(VM, VM, VM),
        scratch_shapes=[
            pltpu.VMEM((CH * TILE, TILE), F32),
            pltpu.SMEM((SLOTS, 64), jnp.int32),
            pltpu.SMEM((1, 64), jnp.int32),
            pltpu.VMEM((ENTRIES, SLOTS, TILE, TILE), BF16),
            pltpu.VMEM((ENTRIES, SLOTS * CH, TILE), BF16),
            pltpu.VMEM((2, CH, TILE), F32),
            pltpu.VMEM((3, CH, TILE), F32),
            DMA((ENTRIES,)), DMA((ENTRIES,)), DMA((ENTRIES,)), DMA((5,)), DMA((5,)), DMA((3,)),
        ],
        compiler_params=pltpu.CompilerParams(
            collective_id=0, has_side_effects=True, vmem_limit_bytes=24 << 20
        ),
        name="remap_send",
    )(*(pltpu.with_memory_space_constraint(a, pltpu.HBM) for a in (cells, weights, source, count)))

    new_state, dm, base, going, grads = network_call(
        ext, cols_in, landed, goal, land, rows_to, diffusivity, coupling.transpose(0, 2, 1),
        b_out.reshape(1, 4), w_in, b_in.reshape(1, HID), w_mid, b_mid.reshape(1, HID), w_out.T,
    )

    adjoint, whole = pl.pallas_call(
        return_body,
        out_shape=(arr((CH * TILE, TILE)), arr((16, PIECE, TILE))),
        in_specs=[VM] * 4 + [HB] + [SM] * 3,
        out_specs=(VM, VM),
        scratch_shapes=[
            pltpu.VMEM((TILE + 2, CH, TILE), F32),
            pltpu.VMEM((ENTRIES, SLOTS, TILE, TILE), BF16),
            pltpu.VMEM((ENTRIES, SLOTS * CH, TILE), BF16),
            pltpu.VMEM((2, CH, TILE), F32),
            pltpu.VMEM((2, CH, TILE), F32),
            pltpu.VMEM((3, CH, TILE), F32),
            pltpu.VMEM((ENTRIES * SLOTS * CH, TILE), F32),
            pltpu.VMEM((TILE, TILE), F32),
            pltpu.VMEM((15, PIECE, TILE), F32),
            pltpu.VMEM((PIECE, TILE), F32),
            pltpu.VMEM((7, PIECE, TILE), F32),
            pltpu.VMEM((PIECE, TILE), F32),
            DMA((ENTRIES,)), DMA((ENTRIES,)), DMA((ENTRIES,)), DMA((5,)), DMA((5,)),
            DMA((15,)), DMA((15,)), DMA((7,)), DMA((7,)), DMA((15,)), DMA((15,)),
        ],
        compiler_params=pltpu.CompilerParams(
            collective_id=1, has_side_effects=True, vmem_limit_bytes=32 << 20
        ),
        name="remap_return",
    )(
        going, dm, base, grads.reshape(16, PIECE, TILE), pltpu.with_memory_space_constraint(weights, pltpu.HBM), source, count, diffusivity
    )
    adjoint, g_w_in, g_b_in, g_w_mid, g_b_mid, g_w_out, g_b_out = pl.pallas_call(
        finish_body,
        out_shape=(
            arr((CH * TILE, TILE)), arr((16, HID)), arr((1, HID)), arr((HID, HID)), arr((1, HID)),
            arr((4, HID)), arr((1, 4)),
        ),
        in_specs=[VM, VM],
        out_specs=(HB,) + (VM,) * 6,
        scratch_shapes=[DMA],
        compiler_params=pltpu.CompilerParams(vmem_limit_bytes=8 << 20),
        name="finish",
    )(adjoint, whole.reshape(16 * PIECE, TILE))
    return (
        new_state.reshape(1, CH, TILE, TILE),
        adjoint.reshape(1, CH, TILE, TILE),
        g_w_in,
        g_b_in.reshape(HID),
        g_w_mid,
        g_b_mid.reshape(HID),
        g_w_out.T,
        g_b_out.reshape(4),
    )


def solution(mesh):
    tiles = P("comp", None, "gy", "gx")
    pairs = P("comp", "gy", "gx")
    return jax.shard_map(
        shards,
        mesh=mesh,
        in_specs=(tiles, tiles, pairs) + (P(),) * 8 + (pairs,) * 4,
        out_specs=(tiles, tiles) + (P(),) * 6,
        check_vma=False,
    )
```

```python
import jax
import jax.numpy as jnp
from jax import lax
from jax.experimental import pallas as pl
from jax.experimental.pallas import tpu as pltpu
from jax.sharding import PartitionSpec as P

MESH = pl.DeviceIdType.MESH
F32 = jnp.float32
BF16 = jnp.bfloat16
ENTRIES = 20
SLOTS = 4
TILE = 128
CH = 8
HID = 256
CHUNK = 8
PIECE = 48
WIDE = 256
SPREAD = (0, 2)
NT = (((1,), (1,)), ((), ()))


def here():
    return lax.axis_index("comp"), lax.axis_index("gy"), lax.axis_index("gx")


def entry(n, i, j):
    top = i // 3
    if n < 15:
        row = top + n // 5
        shift = n % 5 - 2
        col = (j + shift + 16) % 16
        place = (i - row // 3) * 5 + 2 - shift
        return jnp.int32(1), row, col, place
    low = 1 - (i + 3) // 4
    middle = 1 - low - top
    shift, turn = n - 17, n - 16
    col = (middle * (j + shift) + (1 - middle) * (15 - j + turn) + 32) % 16
    apart = ((col - j + 18) % 16 + 11) // 16
    valid = middle + (top * apart if n < 18 else 0)
    place = middle * (i * 5 + 2 - shift) + (1 - middle) * n
    place = place - 5 * middle
    return valid, jnp.int32(3), col, place


def halo_peers(c, i, j):
    return (
        (jnp.int32(1), (c, i, (j + 15) % 16)),
        (jnp.int32(1), (c, i, (j + 1) % 16)),
        ((i + 3) // 4, (c, (i + 3) % 4, j)),
        (1 - i // 3, (c, (i + 1) % 4, j)),
        (c * (i // 3), (c, i, 15 - j)),
    )


def signal_to(barrier, device):
    pl.semaphore_signal(barrier, inc=1, device_id=device, device_id_type=MESH)


def greet(barrier, c, i, j):
    expected = jnp.int32(0)
    for n in range(ENTRIES):
        valid, row, col, _ = entry(n, i, j)
        expected = expected + valid
        if n < 15:
            signal_to(barrier, (1 - c, row, col))
        else:
            pl.when(valid == 1)(lambda row=row, col=col: signal_to(barrier, (1 - c, row, col)))
    for valid, device in halo_peers(c, i, j):
        expected = expected + valid
        pl.when(valid == 1)(lambda device=device: signal_to(barrier, device))
    return expected


def remote(src, dst, send, recv, device):
    return pltpu.make_async_remote_copy(
        src_ref=src, dst_ref=dst, send_sem=send, recv_sem=recv, device_id=device, device_id_type=MESH
    )


def halo_copies(c, i, j, ext, cols_out, cols_in, rows_in, send, recv):
    west, east, south, north, fold = halo_peers(c, i, j)
    return (
        (west[0], remote(cols_out.at[0], cols_in.at[1], send.at[0], recv.at[1], west[1])),
        (east[0], remote(cols_out.at[1], cols_in.at[0], send.at[1], recv.at[0], east[1])),
        (south[0], remote(ext.at[1], rows_in.at[1], send.at[2], recv.at[3], south[1])),
        (north[0], remote(ext.at[TILE], rows_in.at[0], send.at[3], recv.at[2], north[1])),
        (fold[0], remote(ext.at[TILE], rows_in.at[2], send.at[4], recv.at[4], fold[1])),
    )


def start_halo(copies):
    for valid, copy in copies:
        pl.when(valid == 1)(copy.start)


def wait_halo(c, i, j, ext, cols_out, cols_in, rows_in, send, recv):
    west, east, south, north, fold = halo_peers(c, i, j)
    from_west = remote(cols_out.at[0], cols_in.at[0], send.at[0], recv.at[0], west[1])
    from_east = remote(cols_out.at[1], cols_in.at[1], send.at[1], recv.at[1], east[1])
    from_south = remote(ext.at[1], rows_in.at[0], send.at[2], recv.at[2], south[1])
    from_north = remote(ext.at[TILE], rows_in.at[1], send.at[3], recv.at[3], north[1])
    from_fold = remote(ext.at[TILE], rows_in.at[2], send.at[4], recv.at[4], fold[1])
    from_west.wait_recv()
    from_east.wait_recv()

    @pl.when(south[0] == 1)
    def _():
        from_south.wait_recv()
        ext[0] = rows_in[0]

    @pl.when(north[0] == 1)
    def _():
        from_north.wait_recv()
        ext[TILE + 1] = rows_in[1]

    @pl.when(south[0] == 0)
    def _():
        ext[0] = jnp.zeros((CH, TILE), F32)

    @pl.when((north[0] == 0) & (fold[0] == 0))
    def _():
        ext[TILE + 1] = jnp.zeros((CH, TILE), F32)

    @pl.when(fold[0] == 1)
    def _():
        from_fold.wait_recv()
        down = lax.broadcasted_iota(jnp.int32, (TILE, TILE), 0)
        across = lax.broadcasted_iota(jnp.int32, (TILE, TILE), 1)
        turn = (down + across == TILE - 1).astype(F32)
        ext[TILE + 1] = jnp.dot(
            rows_in[2], turn, precision=lax.Precision.HIGHEST, preferred_element_type=F32
        )


def wait_halo_sent(c, i, j, ext, cols_out, cols_in, rows_in, send, recv):
    for valid, copy in halo_copies(c, i, j, ext, cols_out, cols_in, rows_in, send, recv):
        pl.when(valid == 1)(copy.wait_send)


def lanes():
    return lax.broadcasted_iota(jnp.int32, (CH, TILE), 1)


def edge_columns(ext, cols_out):
    lane = lanes()

    firsts, lasts = [jnp.zeros((CH, TILE), F32)] * 4, [jnp.zeros((CH, TILE), F32)] * 4
    for row in range(TILE):
        cells = ext[row + 1]
        k = row % 4
        firsts[k] = jnp.where(lane == row, pltpu.roll(cells, row, 1) if row else cells, firsts[k])
        lasts[k] = jnp.where(lane == row, pltpu.roll(cells, row + 1, 1) if row < TILE - 1 else cells, lasts[k])
    first = (firsts[0] + firsts[1]) + (firsts[2] + firsts[3])
    last = (lasts[0] + lasts[1]) + (lasts[2] + lasts[3])
    cols_out[0] = first
    cols_out[1] = last


def laplace_row(ext, cols_in, row, lane):
    cells = ext[row + 1]
    west = pltpu.roll(jnp.where(lane == TILE - 1, pltpu.roll(cols_in[0], TILE - 1 - row, 1), cells), 1, 1)
    east = pltpu.roll(jnp.where(lane == 0, pltpu.roll(cols_in[1], TILE - row, 1), cells), TILE - 1, 1)
    return east + west + ext[row] + ext[row + 2] - 4.0 * cells


def send_body(state_in, weights, source_in, count_in, ext, cols_in, landed,
              state, source, count, kernels, outgoing, cols_out, rows_in, load_sem, send_sem, recv_sem, hsend_sem, hrecv_sem, in_sem):
    c, i, j = here()
    firsts = [
        pltpu.make_async_copy(given, held, in_sem.at[k])
        for k, (given, held) in enumerate(((state_in, state), (source_in, source), (count_in, count)))
    ]
    for load in firsts:
        load.start()
    barrier = pltpu.get_barrier_semaphore()
    expected = greet(barrier, c, i, j)
    peers = [entry(n, i, j) for n in range(ENTRIES)]
    loads = []
    for n, (_, row, col, _) in enumerate(peers):
        load = pltpu.make_async_copy(weights.at[row * 16 + col], kernels.at[n], load_sem.at[n])
        load.start()
        loads.append(load)
    for load in firsts:
        load.wait()

    def turn(group, carry):
        for k in range(8):
            row = group * 8 + k
            ext[row + 1] = state[pl.ds(row, CH, stride=TILE), :]
        return carry

    lax.fori_loop(0, TILE // 8, turn, 0)
    edge_columns(ext, cols_out)
    halo = (c, i, j, ext, cols_out, cols_in, rows_in, hsend_sem, hrecv_sem)
    sends = []
    for n, (valid, row, col, place) in enumerate(peers):
        sends.append(
            remote(outgoing.at[n], landed.at[place], send_sem.at[n], recv_sem.at[place], (1 - c, row, col))
        )
    for group in range(4):
        members = range(group * 5, group * 5 + 5)
        for n in members:
            loads[n].wait()
        for n in members:
            _, row, col, _ = peers[n]
            tile = row * 16 + col
            live = count[0, tile]
            parts = []
            for s in range(SLOTS):
                keep = (live > s).astype(F32)
                cells = (ext[source[s, tile] + 1] * keep).astype(BF16)
                parts.append(jnp.dot(cells, kernels[n, s], preferred_element_type=F32))
            outgoing[n] = jnp.concatenate(parts, axis=0).astype(BF16)
        if group == 0:
            pl.semaphore_wait(barrier, expected)
            start_halo(halo_copies(*halo))
        for n in members:
            if n < 15:
                sends[n].start()
            else:
                pl.when(peers[n][0] == 1)(sends[n].start)
    wait_halo(*halo)
    for n, (valid, row, col, _) in enumerate(peers):
        arrival = remote(outgoing.at[n], landed.at[n], send_sem.at[n], recv_sem.at[n], (1 - c, row, col))
        if n < 15:
            arrival.wait_recv()
        else:
            pl.when(valid == 1)(arrival.wait_recv)

            @pl.when(valid == 0)
            def _(n=n):
                landed[n] = jnp.zeros((SLOTS * CH, TILE), BF16)

    for n, (valid, _, _, _) in enumerate(peers):
        if n < 15:
            sends[n].wait_send()
        else:
            pl.when(valid == 1)(sends[n].wait_send)
    wait_halo_sent(*halo)


def network_body(ext, cols_in, landed, target, land, rows_to, rate, couple, bias_out,
                 w_in, b_in, w_mid, b_mid, w_out,
                 new_state, dm, base, going, grads,
                 remapped, other_cot, first_w, first_back, mid_turned, mid_half, out_half, w_out_turned, wide_out, mid_bias, g_first, g_mid, g_out, g_bias, *kept):
    c, i, j = here()
    lane = lanes()
    peers = [entry(n, i, j) for n in range(ENTRIES)]
    remapped[...] = jnp.zeros_like(remapped)
    for n, (_, row, col, _) in enumerate(peers):
        tile = row * 16 + col
        block = landed[n].astype(F32)
        for s in range(SLOTS):
            to = rows_to[s, tile]
            remapped[to] = remapped[to] + block[s * CH:(s + 1) * CH]

    flip = c == 1
    given = w_in[...].astype(F32)
    own_w = jnp.where(flip, given[CH:], given[:CH])
    other_w = jnp.where(flip, given[:CH], given[CH:])
    bias = b_in[...]
    high = bias.astype(BF16).astype(F32)
    middle = (bias - high).astype(BF16).astype(F32)
    lower = bias - high - middle
    rows = lax.broadcasted_iota(jnp.int32, (16, HID), 0)
    extra = jnp.where(rows == 0, high, jnp.where(rows == 1, middle, jnp.where(rows == 2, lower, 0.0)))
    first_back[...] = jnp.concatenate([own_w, other_w], axis=0).astype(BF16)
    whole = jnp.concatenate([own_w, other_w, extra, jnp.zeros((TILE - 32, HID), F32)], axis=0)
    first_w[...] = (0.5 * whole.T).astype(BF16)
    mid = w_mid[...].astype(F32) * 0.5
    mid_half[...] = mid.astype(BF16)
    mid_turned[...] = mid.T.astype(BF16)
    tall = jnp.concatenate([w_out[...].astype(F32), jnp.zeros((TILE - 4, HID), F32)], axis=0)
    w_out_turned[...] = tall[:16].astype(BF16)
    out_half[...] = (0.5 * tall.T)[:, :16].astype(BF16)
    for f in range(4):
        wide_out[f] = jnp.broadcast_to(0.5 * tall[f:f + 1], (WIDE, HID)).T
    mid_bias[...] = jnp.broadcast_to(0.5 * b_mid[...], (TILE, HID)).T
    ones = (lax.broadcasted_iota(jnp.int32, (16, WIDE), 0) < 3).astype(BF16)
    for p in range(CHUNK * TILE // WIDE):
        kept[1][HID:, p * WIDE:(p + 1) * WIDE] = ones
        kept[10][HID:, p * WIDE:(p + 1) * WIDE] = ones
    g_first[...] = jnp.zeros_like(g_first)
    g_mid[...] = jnp.zeros_like(g_mid)
    g_out[...] = jnp.zeros_like(g_out)
    g_bias[...] = jnp.zeros_like(g_bias)
    sub = lax.broadcasted_iota(jnp.int32, (CH, TILE), 0)

    def column(scalars):
        out = jnp.zeros((CH, TILE), F32)
        for k, value in enumerate(scalars):
            out = jnp.where(sub == k, value, out)
        return out

    rates = column([rate[c, k] for k in range(CH)])
    pulls = [column([couple[c, f, k] for k in range(CH)]) for f in range(4)]
    out_bias = column([bias_out[0, f] for f in range(4)])

    def forward(start, part, features_ref, hidden_ref, slope_one, slope_two, second_ref, raw_ref, *_):
        span = slice(part * WIDE, (part + 1) * WIDE)
        first_row = start + part * (WIDE // TILE)
        blocks = [
            jnp.concatenate([ext[first_row + k + 1], remapped[first_row + k]], axis=0).astype(BF16)
            for k in range(WIDE // TILE)
        ]
        features = jnp.concatenate([jnp.concatenate(blocks, axis=1), ones], axis=0)
        features_ref[:, span] = features
        half_first = jnp.dot(first_w[:, :32], features, preferred_element_type=F32)
        yield
        tan_first = jnp.tanh(half_first)
        up_first = 1.0 + tan_first
        act_first = half_first * up_first
        slope_one[:, span] = up_first + act_first * (1.0 - tan_first)
        hidden_first = act_first.astype(BF16)
        hidden_ref[:HID, span] = hidden_first
        half_second = jnp.dot(mid_turned[...], hidden_first, preferred_element_type=F32)
        yield
        half_second = half_second + jnp.concatenate([mid_bias[...]] * (WIDE // TILE), axis=1)
        tan_second = jnp.tanh(half_second)
        up_second = 1.0 + tan_second
        act_second = half_second * up_second
        slope_two[:, span] = up_second + act_second * (1.0 - tan_second)
        hidden_second = act_second.astype(BF16)
        second_ref[:, span] = hidden_second
        raw_ref[:, span] = jnp.dot(w_out_turned[...], hidden_second, preferred_element_type=F32)
        yield

    def backward(start, part, features_ref, hidden_ref, slope_one, slope_two, second_ref, raw_ref, one_ref, two_ref, cot_ref):
        span = slice(part * WIDE, (part + 1) * WIDE)
        first_row = start + part * (WIDE // TILE)
        raw = raw_ref[:CH, span]
        misfits, cots = [], []
        for k in range(WIDE // TILE):
            row = first_row + k
            wet = jnp.broadcast_to(land[pl.ds(row, 1), :].astype(F32), (CH, TILE))
            open_sea = jnp.where(flip, wet, 1.0)
            fluxes = (raw[:, k * TILE:(k + 1) * TILE] + out_bias) * wet
            updated = ext[row + 1] + rates * open_sea * laplace_row(ext, cols_in, row, lane)
            for f in range(4):
                updated = updated + pulls[f] * fluxes[f:f + 1]
            new_state[pl.ds(row, CH, stride=TILE), :] = updated
            misfit = updated - target[pl.ds(row, CH, stride=TILE), :]
            misfits.append(misfit)
            dm[row + 1] = misfit * open_sea
            cot = jnp.zeros((CH, TILE), F32)
            for f in range(4):
                cot = jnp.where(sub == f, jnp.sum(pulls[f] * misfit, axis=0, keepdims=True), cot)
            cot = jnp.concatenate([cot * wet, jnp.zeros((CH, TILE), F32)], axis=0).astype(BF16)
            cots.append(cot)
            g_bias[...] += cot.astype(F32)[:CH]
        flux_cot = jnp.concatenate(cots, axis=1)
        cot_ref[:, span] = flux_cot
        if part in SPREAD:
            exact = flux_cot.astype(F32)
            pulled = sum(wide_out[f] * exact[f:f + 1] for f in range(4))
        else:
            pulled = jnp.dot(out_half[...], flux_cot, preferred_element_type=F32)
        yield
        second_cot = (pulled * slope_two[:, span]).astype(BF16)
        two_ref[:, span] = second_cot
        pulled = jnp.dot(mid_half[...], second_cot, preferred_element_type=F32)
        yield
        first_cot = (pulled * slope_one[:, span]).astype(BF16)
        one_ref[:, span] = first_cot
        feature_cot = jnp.dot(first_back[...], first_cot, preferred_element_type=F32)
        yield
        for k in range(WIDE // TILE):
            piece = feature_cot[:, k * TILE:(k + 1) * TILE]
            base[first_row + k] = misfits[k] + piece[:CH]
            other_cot[first_row + k] = piece[CH:]

    def gradients(features_ref, hidden_ref, slope_one, slope_two, second_ref, raw_ref, one_ref, two_ref, cot_ref):
        g_mid[...] += lax.dot_general(hidden_ref[...], two_ref[...], NT, preferred_element_type=F32)
        g_out[...] += lax.dot_general(cot_ref[...], second_ref[...], NT, preferred_element_type=F32)
        g_first[...] += lax.dot_general(features_ref[...], one_ref[...], NT, preferred_element_type=F32)

    def play(*chains):
        while chains:
            chains = [chain for chain in chains if next(chain, chain) is not chain]

    PARTS = CHUNK * TILE // WIDE
    half = len(kept) // 2
    even, odd = kept[:half], kept[half:]
    play(*(forward(0, p, *even) for p in range(PARTS)))

    def both(back_at, back, front_at, front):
        chains = []
        for p in range(PARTS):
            if front is not None:
                chains.append(forward(front_at, p, *front))
            chains.append(backward(back_at, p, *back))
        play(*chains)
        gradients(*back)

    def step(pair, carry):
        at = pair * (2 * CHUNK)
        both(at, even, at + CHUNK, odd)
        both(at + CHUNK, odd, at + 2 * CHUNK, even)
        return carry

    lax.fori_loop(0, TILE // (2 * CHUNK) - 1, step, 0)
    both(TILE - 2 * CHUNK, even, TILE - CHUNK, odd)
    both(TILE - CHUNK, odd, 0, None)
    zero = jnp.zeros((CH, TILE), F32)
    dm[0] = zero
    dm[TILE + 1] = zero
    for n, (_, row, col, _) in enumerate(peers):
        tile = row * 16 + col
        going[n] = jnp.concatenate(
            [other_cot[rows_to[s, tile]] for s in range(SLOTS)], axis=0
        ).astype(BF16)
    def pack(at, values):
        grads[at:at + values.shape[0]] = values.astype(BF16)

    for side in range(2):
        columns = slice(side * TILE, (side + 1) * TILE)
        pack(side * HID, g_mid[:HID, columns])
        own, other, extra = g_first[0:8, columns], g_first[8:16, columns], g_first[16:32, columns]
        pack(512 + side * 16, jnp.concatenate([jnp.where(flip, other, own), jnp.where(flip, own, other)], axis=0))
        pack(544 + side * 16, extra)
        pack(576 + side * 16, g_mid[HID:HID + 16, columns])
        pack(608 + side * 16, g_out[:, columns])
    pack(640, jnp.concatenate([g_bias[...], jnp.zeros((CH, TILE), F32)], axis=0))
    pack(656, jnp.zeros((16 * PIECE - 656, TILE), F32))


def return_body(going, dm_in, base, grads, weights, source, count, rate,
                adjoint, whole,
                dm, kernels, back_in, cols_out, cols_in, rows_in, spread, anchor, first_in, mid_sum, second_in, total,
                load_sem, send_sem, recv_sem, hsend_sem, hrecv_sem, s1, r1, s2, r2, s3, r3):
    c, i, j = here()
    lane = lanes()
    barrier = pltpu.get_barrier_semaphore()
    me = c * 4 + i
    across = [(j + d) % 16 for d in range(1, 16)]
    along = [((me + d) % 8 // 4, (me + d) % 4) for d in range(1, 8)]
    for col in across:
        signal_to(barrier, (c, i, col))
    for other in along:
        signal_to(barrier, (*other, j))
    expected = greet(barrier, c, i, j) + 22
    peers = [entry(n, i, j) for n in range(ENTRIES)]
    loads = []
    for n, (_, row, col, _) in enumerate(peers):
        load = pltpu.make_async_copy(weights.at[row * 16 + col], kernels.at[n], load_sem.at[n])
        load.start()
        loads.append(load)
    pl.semaphore_wait(barrier, expected)
    halo = (c, i, j, dm, cols_out, cols_in, rows_in, hsend_sem, hrecv_sem)
    phase1 = [
        remote(grads.at[col], first_in.at[d], s1.at[d], r1.at[d], (c, i, col)) for d, col in enumerate(across)
    ]
    for copy in phase1:
        copy.start()
    sends = []
    for n, (valid, row, col, place) in enumerate(peers):
        copy = remote(going.at[n], back_in.at[place], send_sem.at[n], recv_sem.at[place], (1 - c, row, col))
        sends.append(copy)
        if n < 15:
            copy.start()
        else:
            pl.when(valid == 1)(copy.start)
    dm[...] = dm_in[...]
    edge_columns(dm, cols_out)
    start_halo(halo_copies(*halo))

    for n, (_, row, col, _) in enumerate(peers):
        tile = row * 16 + col
        live = count[0, tile]
        used = peers[n][0]
        for s in range(SLOTS):
            at = source[s, tile]
            keep = (live > s).astype(F32) * used.astype(F32)
            anchor[pl.ds(n * SLOTS + s, 1), :] = (lane[:1] == at).astype(F32) * keep
    anchor[80:, :] = jnp.zeros((TILE - 80, TILE), F32)
    turned = anchor[...].T[:, :80].astype(BF16)
    both = jnp.concatenate([turned, turned], axis=1)

    for copy in phase1:
        copy.wait_recv()
    partial = grads[j].astype(F32)
    for d in range(15):
        partial = partial + first_in[d].astype(F32)
    mid_sum[...] = partial.astype(BF16)
    second_in[me] = partial.astype(BF16)
    phase2 = [
        remote(mid_sum, second_in.at[me], s2.at[d], r2.at[d], (*other, j)) for d, other in enumerate(along)
    ]
    for copy in phase2:
        copy.start()

    wait_halo(*halo)
    sub = lax.broadcasted_iota(jnp.int32, (CH, TILE), 0)
    rates = jnp.zeros((CH, TILE), F32)
    for k in range(CH):
        rates = jnp.where(sub == k, rate[c, k], rates)

    def step(group, carry):
        for k in range(8):
            row = group * 8 + k
            adjoint[pl.ds(row, CH, stride=TILE), :] = base[row] + rates * laplace_row(dm, cols_in, row, lane)
        return carry

    lax.fori_loop(0, TILE // 8, step, 0)

    for d in range(7):
        remote(mid_sum, second_in.at[(me + 7 - d) % 8], s2.at[d], r2.at[d], (*along[d], j)).wait_recv()
    partial = second_in[0].astype(F32)
    for d in range(1, 8):
        partial = partial + second_in[d].astype(F32)
    total[...] = partial.astype(BF16)
    whole[j] = partial.astype(BF16)
    phase3 = [
        remote(total, whole.at[j], s3.at[d], r3.at[d], (c, i, col)) for d, col in enumerate(across)
    ]
    for copy in phase3:
        copy.start()

    for n, (valid, row, col, _) in enumerate(peers):
        arrival = remote(going.at[n], back_in.at[n], send_sem.at[n], recv_sem.at[n], (1 - c, row, col))
        if n < 15:
            arrival.wait_recv()
        else:
            pl.when(valid == 1)(arrival.wait_recv)

            @pl.when(valid == 0)
            def _(n=n):
                back_in[n] = jnp.zeros((SLOTS * CH, TILE), BF16)

    for n in range(ENTRIES):
        loads[n].wait()
    for n in range(ENTRIES):
        made = lax.dot_general(
            back_in[n], kernels[n].reshape(SLOTS * TILE, TILE), NT, preferred_element_type=F32
        )
        for s in range(SLOTS):
            spread[pl.ds(n * SLOTS + s, CH, stride=80), :] = made[s * CH:(s + 1) * CH, s * TILE:(s + 1) * TILE]
    for ch in range(CH):
        cells = spread[ch * 80:(ch + 1) * 80, :]
        high = cells.astype(BF16)
        low = (cells - high.astype(F32)).astype(BF16)
        adjoint[ch * TILE:(ch + 1) * TILE, :] += jnp.dot(
            both, jnp.concatenate([high, low], axis=0), preferred_element_type=F32
        )

    for d in range(15):
        remote(total, whole.at[(j + 15 - d) % 16], s3.at[d], r3.at[d], (c, i, across[d])).wait_recv()
    for n, (valid, _, _, _) in enumerate(peers):
        if n < 15:
            sends[n].wait_send()
        else:
            pl.when(valid == 1)(sends[n].wait_send)
    wait_halo_sent(*halo)
    for copy in phase1 + phase2 + phase3:
        copy.wait_send()


def finish_body(adjoint_in, whole, adjoint, o_w_in, o_b_in, o_w_mid, o_b_mid, o_w_out, o_b_out, sem):
    copy = pltpu.make_async_copy(adjoint_in, adjoint, sem)
    copy.start()
    flat = whole[...].astype(F32) * (1.0 / 1048576.0)
    for side in range(2):
        columns = slice(side * TILE, (side + 1) * TILE)
        o_w_mid[:, columns] = flat[side * HID:(side + 1) * HID]
        o_w_in[:, columns] = flat[512 + side * 16:528 + side * 16]
        o_b_in[:, columns] = flat[544 + side * 16:545 + side * 16]
        o_b_mid[:, columns] = flat[576 + side * 16:577 + side * 16]
        o_w_out[:, columns] = flat[608 + side * 16:612 + side * 16]
    sums = jnp.broadcast_to(jnp.sum(flat[640:648], axis=1, keepdims=True), (CH, TILE))
    sub = lax.broadcasted_iota(jnp.int32, (CH, TILE), 0)
    picked = jnp.sum(jnp.where(sub == lanes(), sums, 0.0), axis=0, keepdims=True)
    o_b_out[...] = picked[:, :4]
    copy.wait()


VM = pl.BlockSpec(memory_space=pltpu.VMEM)
SM = pl.BlockSpec(memory_space=pltpu.SMEM)
HB = pl.BlockSpec(memory_space=pltpu.HBM)
DMA = pltpu.SemaphoreType.DMA


def arr(shape, dtype=F32):
    return jax.ShapeDtypeStruct(shape, dtype)


def network_call(*args):
    return pl.pallas_call(
        network_body,
        out_shape=(
            arr((CH * TILE, TILE)),
            arr((TILE + 2, CH, TILE)),
            arr((TILE, CH, TILE)),
            arr((ENTRIES, SLOTS * CH, TILE), BF16),
            arr((16 * PIECE, TILE), BF16),
        ),
        in_specs=[VM] * 5 + [SM] * 4 + [VM] * 5,
        out_specs=(VM,) * 5,
        scratch_shapes=[
            pltpu.VMEM((TILE, CH, TILE), F32),
            pltpu.VMEM((TILE, CH, TILE), F32),
            pltpu.VMEM((HID, TILE), BF16),
            pltpu.VMEM((16, HID), BF16),
            pltpu.VMEM((HID, HID), BF16),
            pltpu.VMEM((HID, HID), BF16),
            pltpu.VMEM((HID, 16), BF16),
            pltpu.VMEM((16, HID), BF16),
            pltpu.VMEM((4, HID, WIDE), F32),
            pltpu.VMEM((HID, TILE), F32),
            pltpu.VMEM((32, HID), F32),
            pltpu.VMEM((HID + 16, HID), F32),
            pltpu.VMEM((16, HID), F32),
            pltpu.VMEM((CH, TILE), F32),
        ]
        + [
            pltpu.VMEM((32, CHUNK * TILE), BF16),
            pltpu.VMEM((HID + 16, CHUNK * TILE), BF16),
            pltpu.VMEM((HID, CHUNK * TILE), F32),
            pltpu.VMEM((HID, CHUNK * TILE), F32),
            pltpu.VMEM((HID, CHUNK * TILE), BF16),
            pltpu.VMEM((16, CHUNK * TILE), F32),
            pltpu.VMEM((HID, CHUNK * TILE), BF16),
            pltpu.VMEM((HID, CHUNK * TILE), BF16),
            pltpu.VMEM((16, CHUNK * TILE), BF16),
        ] * 2,
        compiler_params=pltpu.CompilerParams(vmem_limit_bytes=48 << 20),
        name="network",
    )(*args)


def shards(state, target, land_mask, diffusivity, coupling, w_in, b_in, w_mid, b_mid, w_out, b_out,
           remap_weight, remap_source, remap_target, remap_count):
    weights = remap_weight.reshape(64, SLOTS, TILE, TILE)
    source = remap_source.reshape(64, SLOTS).T
    rows_to = remap_target.reshape(64, SLOTS).T
    count = remap_count.reshape(1, 64)
    cells = state.reshape(CH * TILE, TILE)
    goal = target.reshape(CH * TILE, TILE)
    land = land_mask.reshape(TILE, TILE)
    ext, cols_in, landed = pl.pallas_call(
        send_body,
        out_shape=(arr((TILE + 2, CH, TILE)), arr((2, CH, TILE)), arr((ENTRIES, SLOTS * CH, TILE), BF16)),
        in_specs=[HB] * 4,
        out_specs=(VM, VM, VM),
        scratch_shapes=[
            pltpu.VMEM((CH * TILE, TILE), F32),
            pltpu.SMEM((SLOTS, 64), jnp.int32),
            pltpu.SMEM((1, 64), jnp.int32),
            pltpu.VMEM((ENTRIES, SLOTS, TILE, TILE), BF16),
            pltpu.VMEM((ENTRIES, SLOTS * CH, TILE), BF16),
            pltpu.VMEM((2, CH, TILE), F32),
            pltpu.VMEM((3, CH, TILE), F32),
            DMA((ENTRIES,)), DMA((ENTRIES,)), DMA((ENTRIES,)), DMA((5,)), DMA((5,)), DMA((3,)),
        ],
        compiler_params=pltpu.CompilerParams(
            collective_id=0, has_side_effects=True, vmem_limit_bytes=24 << 20
        ),
        name="remap_send",
    )(*(pltpu.with_memory_space_constraint(a, pltpu.HBM) for a in (cells, weights, source, count)))

    new_state, dm, base, going, grads = network_call(
        ext, cols_in, landed, goal, land, rows_to, diffusivity, coupling.transpose(0, 2, 1),
        b_out.reshape(1, 4), w_in, b_in.reshape(1, HID), w_mid, b_mid.reshape(1, HID), w_out.T,
    )

    adjoint, whole = pl.pallas_call(
        return_body,
        out_shape=(arr((CH * TILE, TILE)), arr((16, PIECE, TILE), BF16)),
        in_specs=[VM] * 4 + [HB] + [SM] * 3,
        out_specs=(VM, VM),
        scratch_shapes=[
            pltpu.VMEM((TILE + 2, CH, TILE), F32),
            pltpu.VMEM((ENTRIES, SLOTS, TILE, TILE), BF16),
            pltpu.VMEM((ENTRIES, SLOTS * CH, TILE), BF16),
            pltpu.VMEM((2, CH, TILE), F32),
            pltpu.VMEM((2, CH, TILE), F32),
            pltpu.VMEM((3, CH, TILE), F32),
            pltpu.VMEM((ENTRIES * SLOTS * CH, TILE), F32),
            pltpu.VMEM((TILE, TILE), F32),
            pltpu.VMEM((15, PIECE, TILE), BF16),
            pltpu.VMEM((PIECE, TILE), BF16),
            pltpu.VMEM((8, PIECE, TILE), BF16),
            pltpu.VMEM((PIECE, TILE), BF16),
            DMA((ENTRIES,)), DMA((ENTRIES,)), DMA((ENTRIES,)), DMA((5,)), DMA((5,)),
            DMA((15,)), DMA((15,)), DMA((7,)), DMA((7,)), DMA((15,)), DMA((15,)),
        ],
        compiler_params=pltpu.CompilerParams(
            collective_id=1, has_side_effects=True, vmem_limit_bytes=32 << 20
        ),
        name="remap_return",
    )(
        going, dm, base, grads.reshape(16, PIECE, TILE), pltpu.with_memory_space_constraint(weights, pltpu.HBM), source, count, diffusivity
    )
    adjoint, g_w_in, g_b_in, g_w_mid, g_b_mid, g_w_out, g_b_out = pl.pallas_call(
        finish_body,
        out_shape=(
            arr((CH * TILE, TILE)), arr((16, HID)), arr((1, HID)), arr((HID, HID)), arr((1, HID)),
            arr((4, HID)), arr((1, 4)),
        ),
        in_specs=[VM, VM],
        out_specs=(HB,) + (VM,) * 6,
        scratch_shapes=[DMA],
        compiler_params=pltpu.CompilerParams(vmem_limit_bytes=8 << 20),
        name="finish",
    )(adjoint, whole.reshape(16 * PIECE, TILE))
    return (
        new_state.reshape(1, CH, TILE, TILE),
        adjoint.reshape(1, CH, TILE, TILE),
        g_w_in,
        g_b_in.reshape(HID),
        g_w_mid,
        g_b_mid.reshape(HID),
        g_w_out.T,
        g_b_out.reshape(4),
    )


def solution(mesh):
    tiles = P("comp", None, "gy", "gx")
    pairs = P("comp", "gy", "gx")
    return jax.shard_map(
        shards,
        mesh=mesh,
        in_specs=(tiles, tiles, pairs) + (P(),) * 8 + (pairs,) * 4,
        out_specs=(tiles, tiles) + (P(),) * 6,
        check_vma=False,
    )
```

```python
import jax
import jax.numpy as jnp
from jax import lax
from jax.experimental import pallas as pl
from jax.experimental.pallas import tpu as pltpu
from jax.sharding import PartitionSpec as P

MESH = pl.DeviceIdType.MESH
F32 = jnp.float32
BF16 = jnp.bfloat16
ENTRIES = 20
SLOTS = 4
TILE = 128
CH = 8
HID = 256
CHUNK = 8
PIECE = 48
WIDE = 256
SPREAD = (0, 2)
NT = (((1,), (1,)), ((), ()))


def here():
    return lax.axis_index("comp"), lax.axis_index("gy"), lax.axis_index("gx")


def entry(n, i, j):
    top = i // 3
    if n < 15:
        row = top + n // 5
        shift = n % 5 - 2
        col = (j + shift + 16) % 16
        place = (i - row // 3) * 5 + 2 - shift
        return jnp.int32(1), row, col, place
    low = 1 - (i + 3) // 4
    middle = 1 - low - top
    shift, turn = n - 17, n - 16
    col = (middle * (j + shift) + (1 - middle) * (15 - j + turn) + 32) % 16
    apart = ((col - j + 18) % 16 + 11) // 16
    valid = middle + (top * apart if n < 18 else 0)
    place = middle * (i * 5 + 2 - shift) + (1 - middle) * n
    place = place - 5 * middle
    return valid, jnp.int32(3), col, place


def halo_peers(c, i, j):
    return (
        (jnp.int32(1), (c, i, (j + 15) % 16)),
        (jnp.int32(1), (c, i, (j + 1) % 16)),
        ((i + 3) // 4, (c, (i + 3) % 4, j)),
        (1 - i // 3, (c, (i + 1) % 4, j)),
        (c * (i // 3), (c, i, 15 - j)),
    )


def signal_to(barrier, device):
    pl.semaphore_signal(barrier, inc=1, device_id=device, device_id_type=MESH)


def greet(barrier, c, i, j):
    expected = jnp.int32(0)
    for n in range(ENTRIES):
        valid, row, col, _ = entry(n, i, j)
        expected = expected + valid
        if n < 15:
            signal_to(barrier, (1 - c, row, col))
        else:
            pl.when(valid == 1)(lambda row=row, col=col: signal_to(barrier, (1 - c, row, col)))
    for valid, device in halo_peers(c, i, j):
        expected = expected + valid
        pl.when(valid == 1)(lambda device=device: signal_to(barrier, device))
    return expected


def remote(src, dst, send, recv, device):
    return pltpu.make_async_remote_copy(
        src_ref=src, dst_ref=dst, send_sem=send, recv_sem=recv, device_id=device, device_id_type=MESH
    )


def halo_copies(c, i, j, ext, cols_out, cols_in, rows_in, send, recv):
    west, east, south, north, fold = halo_peers(c, i, j)
    return (
        (west[0], remote(cols_out.at[0], cols_in.at[1], send.at[0], recv.at[1], west[1])),
        (east[0], remote(cols_out.at[1], cols_in.at[0], send.at[1], recv.at[0], east[1])),
        (south[0], remote(ext.at[1], rows_in.at[1], send.at[2], recv.at[3], south[1])),
        (north[0], remote(ext.at[TILE], rows_in.at[0], send.at[3], recv.at[2], north[1])),
        (fold[0], remote(ext.at[TILE], rows_in.at[2], send.at[4], recv.at[4], fold[1])),
    )


def start_halo(copies):
    for valid, copy in copies:
        pl.when(valid == 1)(copy.start)


def wait_halo(c, i, j, ext, cols_out, cols_in, rows_in, send, recv):
    west, east, south, north, fold = halo_peers(c, i, j)
    from_west = remote(cols_out.at[0], cols_in.at[0], send.at[0], recv.at[0], west[1])
    from_east = remote(cols_out.at[1], cols_in.at[1], send.at[1], recv.at[1], east[1])
    from_south = remote(ext.at[1], rows_in.at[0], send.at[2], recv.at[2], south[1])
    from_north = remote(ext.at[TILE], rows_in.at[1], send.at[3], recv.at[3], north[1])
    from_fold = remote(ext.at[TILE], rows_in.at[2], send.at[4], recv.at[4], fold[1])
    from_west.wait_recv()
    from_east.wait_recv()

    @pl.when(south[0] == 1)
    def _():
        from_south.wait_recv()
        ext[0] = rows_in[0]

    @pl.when(north[0] == 1)
    def _():
        from_north.wait_recv()
        ext[TILE + 1] = rows_in[1]

    @pl.when(south[0] == 0)
    def _():
        ext[0] = jnp.zeros((CH, TILE), F32)

    @pl.when((north[0] == 0) & (fold[0] == 0))
    def _():
        ext[TILE + 1] = jnp.zeros((CH, TILE), F32)

    @pl.when(fold[0] == 1)
    def _():
        from_fold.wait_recv()
        down = lax.broadcasted_iota(jnp.int32, (TILE, TILE), 0)
        across = lax.broadcasted_iota(jnp.int32, (TILE, TILE), 1)
        turn = (down + across == TILE - 1).astype(F32)
        ext[TILE + 1] = jnp.dot(
            rows_in[2], turn, precision=lax.Precision.HIGHEST, preferred_element_type=F32
        )


def wait_halo_sent(c, i, j, ext, cols_out, cols_in, rows_in, send, recv):
    for valid, copy in halo_copies(c, i, j, ext, cols_out, cols_in, rows_in, send, recv):
        pl.when(valid == 1)(copy.wait_send)


def lanes():
    return lax.broadcasted_iota(jnp.int32, (CH, TILE), 1)


def edge_columns(ext, cols_out):
    lane = lanes()

    firsts, lasts = [jnp.zeros((CH, TILE), F32)] * 4, [jnp.zeros((CH, TILE), F32)] * 4
    for row in range(TILE):
        cells = ext[row + 1]
        k = row % 4
        firsts[k] = jnp.where(lane == row, pltpu.roll(cells, row, 1) if row else cells, firsts[k])
        lasts[k] = jnp.where(lane == row, pltpu.roll(cells, row + 1, 1) if row < TILE - 1 else cells, lasts[k])
    first = (firsts[0] + firsts[1]) + (firsts[2] + firsts[3])
    last = (lasts[0] + lasts[1]) + (lasts[2] + lasts[3])
    cols_out[0] = first
    cols_out[1] = last


def laplace_row(ext, cols_in, row, lane):
    cells = ext[row + 1]
    west = pltpu.roll(jnp.where(lane == TILE - 1, pltpu.roll(cols_in[0], TILE - 1 - row, 1), cells), 1, 1)
    east = pltpu.roll(jnp.where(lane == 0, pltpu.roll(cols_in[1], TILE - row, 1), cells), TILE - 1, 1)
    return east + west + ext[row] + ext[row + 2] - 4.0 * cells


def send_body(state_in, weights, source_in, count_in, ext, cols_in, landed,
              state, source, count, kernels, outgoing, cols_out, rows_in, load_sem, send_sem, recv_sem, hsend_sem, hrecv_sem, in_sem):
    c, i, j = here()
    firsts = [
        pltpu.make_async_copy(given, held, in_sem.at[k])
        for k, (given, held) in enumerate(((state_in, state), (source_in, source), (count_in, count)))
    ]
    for load in firsts:
        load.start()
    barrier = pltpu.get_barrier_semaphore()
    expected = greet(barrier, c, i, j)
    peers = [entry(n, i, j) for n in range(ENTRIES)]
    loads = []
    for n, (_, row, col, _) in enumerate(peers):
        load = pltpu.make_async_copy(weights.at[row * 16 + col], kernels.at[n], load_sem.at[n])
        load.start()
        loads.append(load)
    for load in firsts:
        load.wait()

    def turn(group, carry):
        for k in range(8):
            row = group * 8 + k
            ext[row + 1] = state[pl.ds(row, CH, stride=TILE), :]
        return carry

    lax.fori_loop(0, TILE // 8, turn, 0)
    edge_columns(ext, cols_out)
    halo = (c, i, j, ext, cols_out, cols_in, rows_in, hsend_sem, hrecv_sem)
    sends = []
    for n, (valid, row, col, place) in enumerate(peers):
        sends.append(
            remote(outgoing.at[n], landed.at[place], send_sem.at[n], recv_sem.at[place], (1 - c, row, col))
        )
    for group in range(4):
        members = range(group * 5, group * 5 + 5)
        for n in members:
            loads[n].wait()
        for n in members:
            _, row, col, _ = peers[n]
            tile = row * 16 + col
            live = count[0, tile]
            parts = []
            for s in range(SLOTS):
                keep = (live > s).astype(F32)
                cells = (ext[source[s, tile] + 1] * keep).astype(BF16)
                parts.append(jnp.dot(cells, kernels[n, s], preferred_element_type=F32))
            outgoing[n] = jnp.concatenate(parts, axis=0).astype(BF16)
        if group == 0:
            pl.semaphore_wait(barrier, expected)
            start_halo(halo_copies(*halo))
        for n in members:
            if n < 15:
                sends[n].start()
            else:
                pl.when(peers[n][0] == 1)(sends[n].start)
    wait_halo(*halo)
    for n, (valid, row, col, _) in enumerate(peers):
        arrival = remote(outgoing.at[n], landed.at[n], send_sem.at[n], recv_sem.at[n], (1 - c, row, col))
        if n < 15:
            arrival.wait_recv()
        else:
            pl.when(valid == 1)(arrival.wait_recv)

            @pl.when(valid == 0)
            def _(n=n):
                landed[n] = jnp.zeros((SLOTS * CH, TILE), BF16)

    for n, (valid, _, _, _) in enumerate(peers):
        if n < 15:
            sends[n].wait_send()
        else:
            pl.when(valid == 1)(sends[n].wait_send)
    wait_halo_sent(*halo)


def network_body(ext, cols_in, landed, target, land, rows_to, rate, couple, bias_out,
                 w_in, b_in, w_mid, b_mid, w_out,
                 new_state, dm, base, going, grads,
                 remapped, other_cot, first_w, first_back, mid_turned, mid_half, out_half, w_out_turned, wide_out, mid_bias, g_first, g_mid, g_out, g_bias, *kept):
    c, i, j = here()
    lane = lanes()
    peers = [entry(n, i, j) for n in range(ENTRIES)]
    remapped[...] = jnp.zeros_like(remapped)
    for n, (_, row, col, _) in enumerate(peers):
        tile = row * 16 + col
        block = landed[n].astype(F32)
        for s in range(SLOTS):
            to = rows_to[s, tile]
            remapped[to] = remapped[to] + block[s * CH:(s + 1) * CH]

    flip = c == 1
    given = w_in[...].astype(F32)
    own_w = jnp.where(flip, given[CH:], given[:CH])
    other_w = jnp.where(flip, given[:CH], given[CH:])
    bias = b_in[...]
    high = bias.astype(BF16).astype(F32)
    middle = (bias - high).astype(BF16).astype(F32)
    lower = bias - high - middle
    rows = lax.broadcasted_iota(jnp.int32, (16, HID), 0)
    extra = jnp.where(rows == 0, high, jnp.where(rows == 1, middle, jnp.where(rows == 2, lower, 0.0)))
    first_back[...] = jnp.concatenate([own_w, other_w], axis=0).astype(BF16)
    whole = jnp.concatenate([own_w, other_w, extra, jnp.zeros((TILE - 32, HID), F32)], axis=0)
    first_w[...] = (0.5 * whole.T).astype(BF16)
    mid = w_mid[...].astype(F32) * 0.5
    mid_half[...] = mid.astype(BF16)
    mid_turned[...] = mid.T.astype(BF16)
    tall = jnp.concatenate([w_out[...].astype(F32), jnp.zeros((TILE - 4, HID), F32)], axis=0)
    w_out_turned[...] = tall[:16].astype(BF16)
    out_half[...] = (0.5 * tall.T)[:, :16].astype(BF16)
    pick = lax.broadcasted_iota(jnp.int32, (16, 4 * TILE), 0) == lax.broadcasted_iota(jnp.int32, (16, 4 * TILE), 1) // TILE
    wide_out[...] = jnp.dot(out_half[...], pick.astype(BF16), preferred_element_type=F32)
    mid_bias[...] = jnp.broadcast_to(0.5 * b_mid[...], (TILE, HID)).T
    ones = (lax.broadcasted_iota(jnp.int32, (16, WIDE), 0) < 3).astype(BF16)
    for p in range(CHUNK * TILE // WIDE):
        kept[1][HID:, p * WIDE:(p + 1) * WIDE] = ones
        kept[10][HID:, p * WIDE:(p + 1) * WIDE] = ones
    g_first[...] = jnp.zeros_like(g_first)
    g_mid[...] = jnp.zeros_like(g_mid)
    g_out[...] = jnp.zeros_like(g_out)
    g_bias[...] = jnp.zeros_like(g_bias)
    sub = lax.broadcasted_iota(jnp.int32, (CH, TILE), 0)

    def column(scalars):
        out = jnp.zeros((CH, TILE), F32)
        for k, value in enumerate(scalars):
            out = jnp.where(sub == k, value, out)
        return out

    rates = column([rate[c, k] for k in range(CH)])
    pulls = [column([couple[c, f, k] for k in range(CH)]) for f in range(4)]
    out_bias = column([bias_out[0, f] for f in range(4)])

    def forward(start, part, features_ref, hidden_ref, slope_one, slope_two, second_ref, raw_ref, *_):
        span = slice(part * WIDE, (part + 1) * WIDE)
        first_row = start + part * (WIDE // TILE)
        blocks = [
            jnp.concatenate([ext[first_row + k + 1], remapped[first_row + k]], axis=0).astype(BF16)
            for k in range(WIDE // TILE)
        ]
        features = jnp.concatenate([jnp.concatenate(blocks, axis=1), ones], axis=0)
        features_ref[:, span] = features
        half_first = jnp.dot(first_w[:, :32], features, preferred_element_type=F32)
        yield
        tan_first = jnp.tanh(half_first)
        up_first = 1.0 + tan_first
        act_first = half_first * up_first
        slope_one[:, span] = up_first + act_first * (1.0 - tan_first)
        hidden_first = act_first.astype(BF16)
        hidden_ref[:HID, span] = hidden_first
        half_second = jnp.dot(mid_turned[...], hidden_first, preferred_element_type=F32)
        yield
        half_second = half_second + jnp.concatenate([mid_bias[...]] * (WIDE // TILE), axis=1)
        tan_second = jnp.tanh(half_second)
        up_second = 1.0 + tan_second
        act_second = half_second * up_second
        slope_two[:, span] = up_second + act_second * (1.0 - tan_second)
        hidden_second = act_second.astype(BF16)
        second_ref[:, span] = hidden_second
        raw_ref[:, span] = jnp.dot(w_out_turned[...], hidden_second, preferred_element_type=F32)
        yield

    def backward(start, part, features_ref, hidden_ref, slope_one, slope_two, second_ref, raw_ref, one_ref, two_ref, cot_ref):
        span = slice(part * WIDE, (part + 1) * WIDE)
        first_row = start + part * (WIDE // TILE)
        raw = raw_ref[:CH, span]
        misfits, cots = [], []
        for k in range(WIDE // TILE):
            row = first_row + k
            wet = jnp.broadcast_to(land[pl.ds(row, 1), :].astype(F32), (CH, TILE))
            open_sea = jnp.where(flip, wet, 1.0)
            fluxes = (raw[:, k * TILE:(k + 1) * TILE] + out_bias) * wet
            updated = ext[row + 1] + rates * open_sea * laplace_row(ext, cols_in, row, lane)
            for f in range(4):
                updated = updated + pulls[f] * fluxes[f:f + 1]
            new_state[pl.ds(row, CH, stride=TILE), :] = updated
            misfit = updated - target[pl.ds(row, CH, stride=TILE), :]
            misfits.append(misfit)
            dm[row + 1] = misfit * open_sea
            cot = jnp.zeros((CH, TILE), F32)
            for f in range(4):
                cot = jnp.where(sub == f, jnp.sum(pulls[f] * misfit, axis=0, keepdims=True), cot)
            cot = jnp.concatenate([cot * wet, jnp.zeros((CH, TILE), F32)], axis=0).astype(BF16)
            cots.append(cot)
            g_bias[...] += cot.astype(F32)[:CH]
        flux_cot = jnp.concatenate(cots, axis=1)
        cot_ref[:, span] = flux_cot
        if part in SPREAD:
            exact = flux_cot.astype(F32)
            pulled = jnp.concatenate(
                [
                    sum(wide_out[:, f * TILE:(f + 1) * TILE] * exact[f:f + 1, k * TILE:(k + 1) * TILE] for f in range(4))
                    for k in range(WIDE // TILE)
                ],
                axis=1,
            )
        else:
            pulled = jnp.dot(out_half[...], flux_cot, preferred_element_type=F32)
        yield
        second_cot = (pulled * slope_two[:, span]).astype(BF16)
        two_ref[:, span] = second_cot
        pulled = jnp.dot(mid_half[...], second_cot, preferred_element_type=F32)
        yield
        first_cot = (pulled * slope_one[:, span]).astype(BF16)
        one_ref[:, span] = first_cot
        feature_cot = jnp.dot(first_back[...], first_cot, preferred_element_type=F32)
        yield
        for k in range(WIDE // TILE):
            piece = feature_cot[:, k * TILE:(k + 1) * TILE]
            base[first_row + k] = misfits[k] + piece[:CH]
            other_cot[first_row + k] = piece[CH:]

    def gradients(features_ref, hidden_ref, slope_one, slope_two, second_ref, raw_ref, one_ref, two_ref, cot_ref):
        g_mid[...] += lax.dot_general(hidden_ref[...], two_ref[...], NT, preferred_element_type=F32)
        g_out[...] += lax.dot_general(cot_ref[...], second_ref[...], NT, preferred_element_type=F32)
        g_first[...] += lax.dot_general(features_ref[...], one_ref[...], NT, preferred_element_type=F32)

    def play(*chains):
        while chains:
            chains = [chain for chain in chains if next(chain, chain) is not chain]

    PARTS = CHUNK * TILE // WIDE
    half = len(kept) // 2
    even, odd = kept[:half], kept[half:]
    play(*(forward(0, p, *even) for p in range(PARTS)))

    def both(back_at, back, front_at, front):
        chains = []
        for p in range(PARTS):
            if front is not None:
                chains.append(forward(front_at, p, *front))
            chains.append(backward(back_at, p, *back))
        play(*chains)
        gradients(*back)

    def step(pair, carry):
        at = pair * (2 * CHUNK)
        both(at, even, at + CHUNK, odd)
        both(at + CHUNK, odd, at + 2 * CHUNK, even)
        return carry

    lax.fori_loop(0, TILE // (2 * CHUNK) - 1, step, 0)
    both(TILE - 2 * CHUNK, even, TILE - CHUNK, odd)
    both(TILE - CHUNK, odd, 0, None)
    zero = jnp.zeros((CH, TILE), F32)
    dm[0] = zero
    dm[TILE + 1] = zero
    for n, (_, row, col, _) in enumerate(peers):
        tile = row * 16 + col
        going[n] = jnp.concatenate(
            [other_cot[rows_to[s, tile]] for s in range(SLOTS)], axis=0
        ).astype(BF16)
    def pack(at, values):
        grads[at:at + values.shape[0]] = values.astype(BF16)

    for side in range(2):
        columns = slice(side * TILE, (side + 1) * TILE)
        pack(side * HID, g_mid[:HID, columns])
        own, other, extra = g_first[0:8, columns], g_first[8:16, columns], g_first[16:32, columns]
        pack(512 + side * 16, jnp.concatenate([jnp.where(flip, other, own), jnp.where(flip, own, other)], axis=0))
        pack(544 + side * 16, extra)
        pack(576 + side * 16, g_mid[HID:HID + 16, columns])
        pack(608 + side * 16, g_out[:, columns])
    pack(640, jnp.concatenate([g_bias[...], jnp.zeros((CH, TILE), F32)], axis=0))
    pack(656, jnp.zeros((16 * PIECE - 656, TILE), F32))


def return_body(going, dm_in, base, grads, weights, source_in, count_in, rate_in,
                adjoint, whole,
                source, count, rate, dm, kernels, back_in, cols_out, cols_in, rows_in, spread, anchor, first_in, mid_sum, second_in, total,
                load_sem, send_sem, recv_sem, hsend_sem, hrecv_sem, s1, r1, s2, r2, s3, r3, in_sem):
    c, i, j = here()
    tables = [
        pltpu.make_async_copy(given, held, in_sem.at[k])
        for k, (given, held) in enumerate(((source_in, source), (count_in, count), (rate_in, rate)))
    ]
    for load in tables:
        load.start()
    lane = lanes()
    barrier = pltpu.get_barrier_semaphore()
    me = c * 4 + i
    across = [(j + d) % 16 for d in range(1, 16)]
    along = [((me + d) % 8 // 4, (me + d) % 4) for d in range(1, 8)]
    for col in across:
        signal_to(barrier, (c, i, col))
    for other in along:
        signal_to(barrier, (*other, j))
    expected = greet(barrier, c, i, j) + 22
    peers = [entry(n, i, j) for n in range(ENTRIES)]
    loads = []
    for n, (_, row, col, _) in enumerate(peers):
        load = pltpu.make_async_copy(weights.at[row * 16 + col], kernels.at[n], load_sem.at[n])
        load.start()
        loads.append(load)
    pl.semaphore_wait(barrier, expected)
    halo = (c, i, j, dm, cols_out, cols_in, rows_in, hsend_sem, hrecv_sem)
    phase1 = [
        remote(grads.at[col], first_in.at[d], s1.at[d], r1.at[d], (c, i, col)) for d, col in enumerate(across)
    ]
    for copy in phase1:
        copy.start()
    sends = []
    for n, (valid, row, col, place) in enumerate(peers):
        copy = remote(going.at[n], back_in.at[place], send_sem.at[n], recv_sem.at[place], (1 - c, row, col))
        sends.append(copy)
        if n < 15:
            copy.start()
        else:
            pl.when(valid == 1)(copy.start)
    dm[...] = dm_in[...]
    edge_columns(dm, cols_out)
    start_halo(halo_copies(*halo))

    for load in tables:
        load.wait()
    for n, (_, row, col, _) in enumerate(peers):
        tile = row * 16 + col
        live = count[0, tile]
        used = peers[n][0]
        for s in range(SLOTS):
            at = source[s, tile]
            keep = (live > s).astype(F32) * used.astype(F32)
            anchor[pl.ds(n * SLOTS + s, 1), :] = (lane[:1] == at).astype(F32) * keep
    anchor[80:, :] = jnp.zeros((TILE - 80, TILE), F32)
    turned = anchor[...].T[:, :80].astype(BF16)
    both = jnp.concatenate([turned, turned], axis=1)

    for copy in phase1:
        copy.wait_recv()
    partial = grads[j].astype(F32)
    for d in range(15):
        partial = partial + first_in[d].astype(F32)
    mid_sum[...] = partial.astype(BF16)
    second_in[me] = partial.astype(BF16)
    phase2 = [
        remote(mid_sum, second_in.at[me], s2.at[d], r2.at[d], (*other, j)) for d, other in enumerate(along)
    ]
    for copy in phase2:
        copy.start()

    wait_halo(*halo)
    sub = lax.broadcasted_iota(jnp.int32, (CH, TILE), 0)
    rates = jnp.zeros((CH, TILE), F32)
    for k in range(CH):
        rates = jnp.where(sub == k, rate[c, k], rates)

    def step(group, carry):
        for k in range(8):
            row = group * 8 + k
            adjoint[pl.ds(row, CH, stride=TILE), :] = base[row] + rates * laplace_row(dm, cols_in, row, lane)
        return carry

    lax.fori_loop(0, TILE // 8, step, 0)

    for d in range(7):
        remote(mid_sum, second_in.at[(me + 7 - d) % 8], s2.at[d], r2.at[d], (*along[d], j)).wait_recv()
    partial = second_in[0].astype(F32)
    for d in range(1, 8):
        partial = partial + second_in[d].astype(F32)
    total[...] = partial.astype(BF16)
    whole[j] = partial.astype(BF16)
    phase3 = [
        remote(total, whole.at[j], s3.at[d], r3.at[d], (c, i, col)) for d, col in enumerate(across)
    ]
    for copy in phase3:
        copy.start()

    for n, (valid, row, col, _) in enumerate(peers):
        arrival = remote(going.at[n], back_in.at[n], send_sem.at[n], recv_sem.at[n], (1 - c, row, col))
        if n < 15:
            arrival.wait_recv()
        else:
            pl.when(valid == 1)(arrival.wait_recv)

            @pl.when(valid == 0)
            def _(n=n):
                back_in[n] = jnp.zeros((SLOTS * CH, TILE), BF16)

    for n in range(ENTRIES):
        loads[n].wait()
    for n in range(ENTRIES):
        made = lax.dot_general(
            back_in[n], kernels[n].reshape(SLOTS * TILE, TILE), NT, preferred_element_type=F32
        )
        for s in range(SLOTS):
            spread[pl.ds(n * SLOTS + s, CH, stride=80), :] = made[s * CH:(s + 1) * CH, s * TILE:(s + 1) * TILE]
    for ch in range(CH):
        cells = spread[ch * 80:(ch + 1) * 80, :]
        high = cells.astype(BF16)
        low = (cells - high.astype(F32)).astype(BF16)
        adjoint[ch * TILE:(ch + 1) * TILE, :] += jnp.dot(
            both, jnp.concatenate([high, low], axis=0), preferred_element_type=F32
        )

    for d in range(15):
        remote(total, whole.at[(j + 15 - d) % 16], s3.at[d], r3.at[d], (c, i, across[d])).wait_recv()
    for n, (valid, _, _, _) in enumerate(peers):
        if n < 15:
            sends[n].wait_send()
        else:
            pl.when(valid == 1)(sends[n].wait_send)
    wait_halo_sent(*halo)
    for copy in phase1 + phase2 + phase3:
        copy.wait_send()


def finish_body(adjoint_in, state_in, whole, adjoint, new_state, o_w_in, o_b_in, o_w_mid, o_b_mid, o_w_out, o_b_out, sem):
    copies = [
        pltpu.make_async_copy(adjoint_in, adjoint, sem.at[0]), pltpu.make_async_copy(state_in, new_state, sem.at[1])
    ]
    for copy in copies:
        copy.start()
    flat = whole[...].astype(F32) * (1.0 / 1048576.0)
    for side in range(2):
        columns = slice(side * TILE, (side + 1) * TILE)
        o_w_mid[:, columns] = flat[side * HID:(side + 1) * HID]
        o_w_in[:, columns] = flat[512 + side * 16:528 + side * 16]
        o_b_in[:, columns] = flat[544 + side * 16:545 + side * 16]
        o_b_mid[:, columns] = flat[576 + side * 16:577 + side * 16]
        o_w_out[:, columns] = flat[608 + side * 16:612 + side * 16]
    sums = jnp.broadcast_to(jnp.sum(flat[640:648], axis=1, keepdims=True), (CH, TILE))
    sub = lax.broadcasted_iota(jnp.int32, (CH, TILE), 0)
    picked = jnp.sum(jnp.where(sub == lanes(), sums, 0.0), axis=0, keepdims=True)
    o_b_out[...] = picked[:, :4]
    for copy in copies:
        copy.wait()


VM = pl.BlockSpec(memory_space=pltpu.VMEM)
SM = pl.BlockSpec(memory_space=pltpu.SMEM)
HB = pl.BlockSpec(memory_space=pltpu.HBM)
DMA = pltpu.SemaphoreType.DMA


def arr(shape, dtype=F32):
    return jax.ShapeDtypeStruct(shape, dtype)


def network_call(*args):
    return pl.pallas_call(
        network_body,
        out_shape=(
            arr((CH * TILE, TILE)),
            arr((TILE + 2, CH, TILE)),
            arr((TILE, CH, TILE)),
            arr((ENTRIES, SLOTS * CH, TILE), BF16),
            arr((16 * PIECE, TILE), BF16),
        ),
        in_specs=[VM] * 5 + [SM] * 4 + [VM] * 5,
        out_specs=(VM,) * 5,
        scratch_shapes=[
            pltpu.VMEM((TILE, CH, TILE), F32),
            pltpu.VMEM((TILE, CH, TILE), F32),
            pltpu.VMEM((HID, TILE), BF16),
            pltpu.VMEM((16, HID), BF16),
            pltpu.VMEM((HID, HID), BF16),
            pltpu.VMEM((HID, HID), BF16),
            pltpu.VMEM((HID, 16), BF16),
            pltpu.VMEM((16, HID), BF16),
            pltpu.VMEM((HID, 4 * TILE), F32),
            pltpu.VMEM((HID, TILE), F32),
            pltpu.VMEM((32, HID), F32),
            pltpu.VMEM((HID + 16, HID), F32),
            pltpu.VMEM((16, HID), F32),
            pltpu.VMEM((CH, TILE), F32),
        ]
        + [
            pltpu.VMEM((32, CHUNK * TILE), BF16),
            pltpu.VMEM((HID + 16, CHUNK * TILE), BF16),
            pltpu.VMEM((HID, CHUNK * TILE), F32),
            pltpu.VMEM((HID, CHUNK * TILE), F32),
            pltpu.VMEM((HID, CHUNK * TILE), BF16),
            pltpu.VMEM((16, CHUNK * TILE), F32),
            pltpu.VMEM((HID, CHUNK * TILE), BF16),
            pltpu.VMEM((HID, CHUNK * TILE), BF16),
            pltpu.VMEM((16, CHUNK * TILE), BF16),
        ] * 2,
        compiler_params=pltpu.CompilerParams(vmem_limit_bytes=48 << 20),
        name="network",
    )(*args)


def shards(state, target, land_mask, diffusivity, coupling, w_in, b_in, w_mid, b_mid, w_out, b_out,
           remap_weight, remap_source, remap_target, remap_count):
    weights = remap_weight.reshape(64, SLOTS, TILE, TILE)
    source = remap_source.reshape(64, SLOTS).T
    rows_to = remap_target.reshape(64, SLOTS).T
    count = remap_count.reshape(1, 64)
    cells = state.reshape(CH * TILE, TILE)
    goal = target.reshape(CH * TILE, TILE)
    land = land_mask.reshape(TILE, TILE)
    ext, cols_in, landed = pl.pallas_call(
        send_body,
        out_shape=(arr((TILE + 2, CH, TILE)), arr((2, CH, TILE)), arr((ENTRIES, SLOTS * CH, TILE), BF16)),
        in_specs=[HB] * 4,
        out_specs=(VM, VM, VM),
        scratch_shapes=[
            pltpu.VMEM((CH * TILE, TILE), F32),
            pltpu.SMEM((SLOTS, 64), jnp.int32),
            pltpu.SMEM((1, 64), jnp.int32),
            pltpu.VMEM((ENTRIES, SLOTS, TILE, TILE), BF16),
            pltpu.VMEM((ENTRIES, SLOTS * CH, TILE), BF16),
            pltpu.VMEM((2, CH, TILE), F32),
            pltpu.VMEM((3, CH, TILE), F32),
            DMA((ENTRIES,)), DMA((ENTRIES,)), DMA((ENTRIES,)), DMA((5,)), DMA((5,)), DMA((3,)),
        ],
        compiler_params=pltpu.CompilerParams(
            collective_id=0, has_side_effects=True, vmem_limit_bytes=24 << 20
        ),
        name="remap_send",
    )(*(pltpu.with_memory_space_constraint(a, pltpu.HBM) for a in (cells, weights, source, count)))

    new_state, dm, base, going, grads = network_call(
        ext, cols_in, landed, goal, land, rows_to, diffusivity, coupling.transpose(0, 2, 1),
        b_out.reshape(1, 4), w_in, b_in.reshape(1, HID), w_mid, b_mid.reshape(1, HID), w_out.T,
    )

    adjoint, whole = pl.pallas_call(
        return_body,
        out_shape=(arr((CH * TILE, TILE)), arr((16, PIECE, TILE), BF16)),
        in_specs=[VM] * 4 + [HB] * 4,
        out_specs=(VM, VM),
        scratch_shapes=[
            pltpu.SMEM((SLOTS, 64), jnp.int32),
            pltpu.SMEM((1, 64), jnp.int32),
            pltpu.SMEM((2, CH), F32),
            pltpu.VMEM((TILE + 2, CH, TILE), F32),
            pltpu.VMEM((ENTRIES, SLOTS, TILE, TILE), BF16),
            pltpu.VMEM((ENTRIES, SLOTS * CH, TILE), BF16),
            pltpu.VMEM((2, CH, TILE), F32),
            pltpu.VMEM((2, CH, TILE), F32),
            pltpu.VMEM((3, CH, TILE), F32),
            pltpu.VMEM((ENTRIES * SLOTS * CH, TILE), F32),
            pltpu.VMEM((TILE, TILE), F32),
            pltpu.VMEM((15, PIECE, TILE), BF16),
            pltpu.VMEM((PIECE, TILE), BF16),
            pltpu.VMEM((8, PIECE, TILE), BF16),
            pltpu.VMEM((PIECE, TILE), BF16),
            DMA((ENTRIES,)), DMA((ENTRIES,)), DMA((ENTRIES,)), DMA((5,)), DMA((5,)),
            DMA((15,)), DMA((15,)), DMA((7,)), DMA((7,)), DMA((15,)), DMA((15,)), DMA((3,)),
        ],
        compiler_params=pltpu.CompilerParams(
            collective_id=1, has_side_effects=True, vmem_limit_bytes=32 << 20
        ),
        name="remap_return",
    )(
        going, dm, base, grads.reshape(16, PIECE, TILE), *(pltpu.with_memory_space_constraint(a, pltpu.HBM) for a in (weights, source, count, diffusivity))
    )
    adjoint, new_state, g_w_in, g_b_in, g_w_mid, g_b_mid, g_w_out, g_b_out = pl.pallas_call(
        finish_body,
        out_shape=(
            arr((CH * TILE, TILE)), arr((CH * TILE, TILE)), arr((16, HID)), arr((1, HID)), arr((HID, HID)), arr((1, HID)),
            arr((4, HID)), arr((1, 4)),
        ),
        in_specs=[VM, VM, VM],
        out_specs=(HB, HB) + (VM,) * 6,
        scratch_shapes=[DMA((2,))],
        compiler_params=pltpu.CompilerParams(vmem_limit_bytes=8 << 20),
        name="finish",
    )(adjoint, new_state, whole.reshape(16 * PIECE, TILE))
    return (
        new_state.reshape(1, CH, TILE, TILE),
        adjoint.reshape(1, CH, TILE, TILE),
        g_w_in,
        g_b_in.reshape(HID),
        g_w_mid,
        g_b_mid.reshape(HID),
        g_w_out.T,
        g_b_out.reshape(4),
    )


def solution(mesh):
    tiles = P("comp", None, "gy", "gx")
    pairs = P("comp", "gy", "gx")
    return jax.shard_map(
        shards,
        mesh=mesh,
        in_specs=(tiles, tiles, pairs) + (P(),) * 8 + (pairs,) * 4,
        out_specs=(tiles, tiles) + (P(),) * 6,
        check_vma=False,
    )
```

```python
import jax
import jax.numpy as jnp
from jax import lax
from jax.experimental import pallas as pl
from jax.experimental.pallas import tpu as pltpu
from jax.sharding import PartitionSpec as P

MESH = pl.DeviceIdType.MESH
F32 = jnp.float32
BF16 = jnp.bfloat16
ENTRIES = 20
SLOTS = 4
TILE = 128
CH = 8
HID = 256
CHUNK = 8
PIECE = 48
WIDE = 256
SPREAD = (0, 2)
NT = (((1,), (1,)), ((), ()))


def here():
    return lax.axis_index("comp"), lax.axis_index("gy"), lax.axis_index("gx")


def entry(n, i, j):
    top = i // 3
    if n < 15:
        row = top + n // 5
        shift = n % 5 - 2
        col = (j + shift + 16) % 16
        place = (i - row // 3) * 5 + 2 - shift
        return jnp.int32(1), row, col, place
    low = 1 - (i + 3) // 4
    middle = 1 - low - top
    shift, turn = n - 17, n - 16
    col = (middle * (j + shift) + (1 - middle) * (15 - j + turn) + 32) % 16
    apart = ((col - j + 18) % 16 + 11) // 16
    valid = middle + (top * apart if n < 18 else 0)
    place = middle * (i * 5 + 2 - shift) + (1 - middle) * n
    place = place - 5 * middle
    return valid, jnp.int32(3), col, place


def halo_peers(c, i, j):
    return (
        (jnp.int32(1), (c, i, (j + 15) % 16)),
        (jnp.int32(1), (c, i, (j + 1) % 16)),
        ((i + 3) // 4, (c, (i + 3) % 4, j)),
        (1 - i // 3, (c, (i + 1) % 4, j)),
        (c * (i // 3), (c, i, 15 - j)),
    )


def signal_to(barrier, device):
    pl.semaphore_signal(barrier, inc=1, device_id=device, device_id_type=MESH)


def greet(barrier, c, i, j):
    expected = jnp.int32(0)
    for n in range(ENTRIES):
        valid, row, col, _ = entry(n, i, j)
        expected = expected + valid
        if n < 15:
            signal_to(barrier, (1 - c, row, col))
        else:
            pl.when(valid == 1)(lambda row=row, col=col: signal_to(barrier, (1 - c, row, col)))
    for valid, device in halo_peers(c, i, j):
        expected = expected + valid
        pl.when(valid == 1)(lambda device=device: signal_to(barrier, device))
    return expected


def remote(src, dst, send, recv, device):
    return pltpu.make_async_remote_copy(
        src_ref=src, dst_ref=dst, send_sem=send, recv_sem=recv, device_id=device, device_id_type=MESH
    )


def halo_copies(c, i, j, ext, cols_out, cols_in, rows_in, send, recv):
    west, east, south, north, fold = halo_peers(c, i, j)
    return (
        (west[0], remote(cols_out.at[0], cols_in.at[1], send.at[0], recv.at[1], west[1])),
        (east[0], remote(cols_out.at[1], cols_in.at[0], send.at[1], recv.at[0], east[1])),
        (south[0], remote(ext.at[1], rows_in.at[1], send.at[2], recv.at[3], south[1])),
        (north[0], remote(ext.at[TILE], rows_in.at[0], send.at[3], recv.at[2], north[1])),
        (fold[0], remote(ext.at[TILE], rows_in.at[2], send.at[4], recv.at[4], fold[1])),
    )


def start_halo(copies):
    for valid, copy in copies:
        pl.when(valid == 1)(copy.start)


def wait_halo(c, i, j, ext, cols_out, cols_in, rows_in, send, recv):
    west, east, south, north, fold = halo_peers(c, i, j)
    from_west = remote(cols_out.at[0], cols_in.at[0], send.at[0], recv.at[0], west[1])
    from_east = remote(cols_out.at[1], cols_in.at[1], send.at[1], recv.at[1], east[1])
    from_south = remote(ext.at[1], rows_in.at[0], send.at[2], recv.at[2], south[1])
    from_north = remote(ext.at[TILE], rows_in.at[1], send.at[3], recv.at[3], north[1])
    from_fold = remote(ext.at[TILE], rows_in.at[2], send.at[4], recv.at[4], fold[1])
    from_west.wait_recv()
    from_east.wait_recv()

    @pl.when(south[0] == 1)
    def _():
        from_south.wait_recv()
        ext[0] = rows_in[0]

    @pl.when(north[0] == 1)
    def _():
        from_north.wait_recv()
        ext[TILE + 1] = rows_in[1]

    @pl.when(south[0] == 0)
    def _():
        ext[0] = jnp.zeros((CH, TILE), F32)

    @pl.when((north[0] == 0) & (fold[0] == 0))
    def _():
        ext[TILE + 1] = jnp.zeros((CH, TILE), F32)

    @pl.when(fold[0] == 1)
    def _():
        from_fold.wait_recv()
        down = lax.broadcasted_iota(jnp.int32, (TILE, TILE), 0)
        across = lax.broadcasted_iota(jnp.int32, (TILE, TILE), 1)
        turn = (down + across == TILE - 1).astype(F32)
        ext[TILE + 1] = jnp.dot(
            rows_in[2], turn, precision=lax.Precision.HIGHEST, preferred_element_type=F32
        )


def wait_halo_sent(c, i, j, ext, cols_out, cols_in, rows_in, send, recv):
    for valid, copy in halo_copies(c, i, j, ext, cols_out, cols_in, rows_in, send, recv):
        pl.when(valid == 1)(copy.wait_send)


def lanes():
    return lax.broadcasted_iota(jnp.int32, (CH, TILE), 1)


def edge_columns(ext, cols_out):
    lane = lanes()

    firsts, lasts = [jnp.zeros((CH, TILE), F32)] * 4, [jnp.zeros((CH, TILE), F32)] * 4
    for row in range(TILE):
        cells = ext[row + 1]
        k = row % 4
        firsts[k] = jnp.where(lane == row, pltpu.roll(cells, row, 1) if row else cells, firsts[k])
        lasts[k] = jnp.where(lane == row, pltpu.roll(cells, row + 1, 1) if row < TILE - 1 else cells, lasts[k])
    first = (firsts[0] + firsts[1]) + (firsts[2] + firsts[3])
    last = (lasts[0] + lasts[1]) + (lasts[2] + lasts[3])
    cols_out[0] = first
    cols_out[1] = last


def laplace_row(ext, cols_in, row, lane):
    cells = ext[row + 1]
    west = pltpu.roll(jnp.where(lane == TILE - 1, pltpu.roll(cols_in[0], TILE - 1 - row, 1), cells), 1, 1)
    east = pltpu.roll(jnp.where(lane == 0, pltpu.roll(cols_in[1], TILE - row, 1), cells), TILE - 1, 1)
    return east + west + ext[row] + ext[row + 2] - 4.0 * cells


def send_body(state_in, weights, source_in, count_in, ext, cols_in, landed,
              state, source, count, kernels, outgoing, cols_out, rows_in, load_sem, send_sem, recv_sem, hsend_sem, hrecv_sem, in_sem):
    c, i, j = here()
    firsts = [
        pltpu.make_async_copy(given, held, in_sem.at[k])
        for k, (given, held) in enumerate(((state_in, state), (source_in, source), (count_in, count)))
    ]
    for load in firsts:
        load.start()
    barrier = pltpu.get_barrier_semaphore()
    expected = greet(barrier, c, i, j)
    peers = [entry(n, i, j) for n in range(ENTRIES)]
    loads = []
    for n, (_, row, col, _) in enumerate(peers):
        load = pltpu.make_async_copy(weights.at[row * 16 + col], kernels.at[n], load_sem.at[n])
        load.start()
        loads.append(load)
    for load in firsts:
        load.wait()

    def turn(group, carry):
        for k in range(8):
            row = group * 8 + k
            ext[row + 1] = state[pl.ds(row, CH, stride=TILE), :]
        return carry

    lax.fori_loop(0, TILE // 8, turn, 0)
    edge_columns(ext, cols_out)
    halo = (c, i, j, ext, cols_out, cols_in, rows_in, hsend_sem, hrecv_sem)
    sends = []
    for n, (valid, row, col, place) in enumerate(peers):
        sends.append(
            remote(outgoing.at[n], landed.at[place], send_sem.at[n], recv_sem.at[place], (1 - c, row, col))
        )
    for group in range(4):
        members = range(group * 5, group * 5 + 5)
        for n in members:
            loads[n].wait()
        for n in members:
            _, row, col, _ = peers[n]
            tile = row * 16 + col
            live = count[0, tile]
            parts = []
            for s in range(SLOTS):
                keep = (live > s).astype(F32)
                cells = (ext[source[s, tile] + 1] * keep).astype(BF16)
                parts.append(jnp.dot(cells, kernels[n, s], preferred_element_type=F32))
            outgoing[n] = jnp.concatenate(parts, axis=0).astype(BF16)
        if group == 0:
            pl.semaphore_wait(barrier, expected)
            start_halo(halo_copies(*halo))
        for n in members:
            if n < 15:
                sends[n].start()
            else:
                pl.when(peers[n][0] == 1)(sends[n].start)
    wait_halo(*halo)
    for n, (valid, row, col, _) in enumerate(peers):
        arrival = remote(outgoing.at[n], landed.at[n], send_sem.at[n], recv_sem.at[n], (1 - c, row, col))
        if n < 15:
            arrival.wait_recv()
        else:
            pl.when(valid == 1)(arrival.wait_recv)

            @pl.when(valid == 0)
            def _(n=n):
                landed[n] = jnp.zeros((SLOTS * CH, TILE), BF16)

    for n, (valid, _, _, _) in enumerate(peers):
        if n < 15:
            sends[n].wait_send()
        else:
            pl.when(valid == 1)(sends[n].wait_send)
    wait_halo_sent(*halo)


def network_body(ext, cols_in, landed, target, land, rows_to, rate, couple, bias_out,
                 w_in, b_in, w_mid, b_mid, w_out,
                 new_state, dm, base, going, grads,
                 remapped, other_cot, first_w, first_back, mid_turned, mid_half, out_half, w_out_turned, wide_out, mid_bias, g_first, g_mid, g_out, g_bias, *kept):
    c, i, j = here()
    lane = lanes()
    peers = [entry(n, i, j) for n in range(ENTRIES)]
    remapped[...] = jnp.zeros_like(remapped)
    for n, (_, row, col, _) in enumerate(peers):
        tile = row * 16 + col
        block = landed[n].astype(F32)
        for s in range(SLOTS):
            to = rows_to[s, tile]
            remapped[to] = remapped[to] + block[s * CH:(s + 1) * CH]

    flip = c == 1
    given = w_in[...].astype(F32)
    own_w = jnp.where(flip, given[CH:], given[:CH])
    other_w = jnp.where(flip, given[:CH], given[CH:])
    bias = b_in[...]
    high = bias.astype(BF16).astype(F32)
    middle = (bias - high).astype(BF16).astype(F32)
    lower = bias - high - middle
    rows = lax.broadcasted_iota(jnp.int32, (16, HID), 0)
    extra = jnp.where(rows == 0, high, jnp.where(rows == 1, middle, jnp.where(rows == 2, lower, 0.0)))
    first_back[...] = jnp.concatenate([own_w, other_w], axis=0).astype(BF16)
    whole = jnp.concatenate([own_w, other_w, extra, jnp.zeros((TILE - 32, HID), F32)], axis=0)
    first_w[...] = (0.5 * whole.T).astype(BF16)
    mid = w_mid[...].astype(F32) * 0.5
    mid_half[...] = mid.astype(BF16)
    mid_turned[...] = mid.T.astype(BF16)
    tall = jnp.concatenate([w_out[...].astype(F32), jnp.zeros((TILE - 4, HID), F32)], axis=0)
    w_out_turned[...] = tall[:16].astype(BF16)
    out_half[...] = (0.5 * tall.T)[:, :16].astype(BF16)
    pick = lax.broadcasted_iota(jnp.int32, (16, 4 * TILE), 0) == lax.broadcasted_iota(jnp.int32, (16, 4 * TILE), 1) // TILE
    wide_out[...] = jnp.dot(out_half[...], pick.astype(BF16), preferred_element_type=F32)
    mid_bias[...] = jnp.broadcast_to(0.5 * b_mid[...], (TILE, HID)).T
    ones = (lax.broadcasted_iota(jnp.int32, (16, WIDE), 0) < 3).astype(BF16)
    for p in range(CHUNK * TILE // WIDE):
        kept[1][HID:, p * WIDE:(p + 1) * WIDE] = ones
        kept[10][HID:, p * WIDE:(p + 1) * WIDE] = ones
    g_first[...] = jnp.zeros_like(g_first)
    g_mid[...] = jnp.zeros_like(g_mid)
    g_out[...] = jnp.zeros_like(g_out)
    g_bias[...] = jnp.zeros_like(g_bias)
    sub = lax.broadcasted_iota(jnp.int32, (CH, TILE), 0)

    def column(scalars):
        out = jnp.zeros((CH, TILE), F32)
        for k, value in enumerate(scalars):
            out = jnp.where(sub == k, value, out)
        return out

    rates = column([rate[c, k] for k in range(CH)])
    pulls = [column([couple[c, f, k] for k in range(CH)]) for f in range(4)]
    out_bias = column([bias_out[0, f] for f in range(4)])

    def forward(start, part, features_ref, hidden_ref, slope_one, slope_two, second_ref, raw_ref, *_):
        span = slice(part * WIDE, (part + 1) * WIDE)
        first_row = start + part * (WIDE // TILE)
        blocks = [
            jnp.concatenate([ext[first_row + k + 1], remapped[first_row + k]], axis=0).astype(BF16)
            for k in range(WIDE // TILE)
        ]
        features = jnp.concatenate([jnp.concatenate(blocks, axis=1), ones], axis=0)
        features_ref[:, span] = features
        half_first = jnp.dot(first_w[:, :32], features, preferred_element_type=F32)
        yield
        tan_first = jnp.tanh(half_first)
        up_first = 1.0 + tan_first
        act_first = half_first * up_first
        slope_one[:, span] = up_first + act_first * (1.0 - tan_first)
        hidden_first = act_first.astype(BF16)
        hidden_ref[:HID, span] = hidden_first
        half_second = jnp.dot(mid_turned[...], hidden_first, preferred_element_type=F32)
        yield
        half_second = half_second + jnp.concatenate([mid_bias[...]] * (WIDE // TILE), axis=1)
        tan_second = jnp.tanh(half_second)
        up_second = 1.0 + tan_second
        act_second = half_second * up_second
        slope_two[:, span] = up_second + act_second * (1.0 - tan_second)
        hidden_second = act_second.astype(BF16)
        second_ref[:, span] = hidden_second
        raw_ref[:, span] = jnp.dot(w_out_turned[...], hidden_second, preferred_element_type=F32)
        yield

    def backward(start, part, features_ref, hidden_ref, slope_one, slope_two, second_ref, raw_ref, one_ref, two_ref, cot_ref):
        span = slice(part * WIDE, (part + 1) * WIDE)
        first_row = start + part * (WIDE // TILE)
        raw = raw_ref[:CH, span]
        misfits, cots = [], []
        for k in range(WIDE // TILE):
            row = first_row + k
            wet = jnp.broadcast_to(land[pl.ds(row, 1), :].astype(F32), (CH, TILE))
            open_sea = jnp.where(flip, wet, 1.0)
            fluxes = (raw[:, k * TILE:(k + 1) * TILE] + out_bias) * wet
            updated = ext[row + 1] + rates * open_sea * laplace_row(ext, cols_in, row, lane)
            for f in range(4):
                updated = updated + pulls[f] * fluxes[f:f + 1]
            new_state[pl.ds(row, CH, stride=TILE), :] = updated
            misfit = updated - target[pl.ds(row, CH, stride=TILE), :]
            misfits.append(misfit)
            dm[row + 1] = misfit * open_sea
            cot = jnp.zeros((CH, TILE), F32)
            for f in range(4):
                cot = jnp.where(sub == f, jnp.sum(pulls[f] * misfit, axis=0, keepdims=True), cot)
            cot = jnp.concatenate([cot * wet, jnp.zeros((CH, TILE), F32)], axis=0).astype(BF16)
            cots.append(cot)
            g_bias[...] += cot.astype(F32)[:CH]
        flux_cot = jnp.concatenate(cots, axis=1)
        cot_ref[:, span] = flux_cot
        if part in SPREAD:
            exact = flux_cot.astype(F32)
            pulled = jnp.concatenate(
                [
                    sum(wide_out[:, f * TILE:(f + 1) * TILE] * exact[f:f + 1, k * TILE:(k + 1) * TILE] for f in range(4))
                    for k in range(WIDE // TILE)
                ],
                axis=1,
            )
        else:
            pulled = jnp.dot(out_half[...], flux_cot, preferred_element_type=F32)
        yield
        second_cot = (pulled * slope_two[:, span]).astype(BF16)
        two_ref[:, span] = second_cot
        pulled = jnp.dot(mid_half[...], second_cot, preferred_element_type=F32)
        yield
        first_cot = (pulled * slope_one[:, span]).astype(BF16)
        one_ref[:, span] = first_cot
        feature_cot = jnp.dot(first_back[...], first_cot, preferred_element_type=F32)
        yield
        for k in range(WIDE // TILE):
            piece = feature_cot[:, k * TILE:(k + 1) * TILE]
            base[first_row + k] = misfits[k] + piece[:CH]
            other_cot[first_row + k] = piece[CH:]

    def gradients(features_ref, hidden_ref, slope_one, slope_two, second_ref, raw_ref, one_ref, two_ref, cot_ref):
        g_out[...] += lax.dot_general(cot_ref[...], second_ref[...], NT, preferred_element_type=F32)
        yield
        g_mid[...] += lax.dot_general(hidden_ref[...], two_ref[...], NT, preferred_element_type=F32)
        yield
        g_first[...] += lax.dot_general(features_ref[...], one_ref[...], NT, preferred_element_type=F32)
        yield

    def play(*chains):
        chains = list(chains)
        while chains:
            chains = [chain for chain in chains if next(chain, chain) is not chain]

    PARTS = CHUNK * TILE // WIDE
    half = len(kept) // 2
    even, odd = kept[:half], kept[half:]
    play(*(forward(0, p, *even) for p in range(PARTS)))

    def both(back_at, back, front_at, front):
        chains = []
        for p in range(PARTS):
            chains.append(backward(back_at, p, *back))
            if front is not None:
                chains.append(forward(front_at, p, *front))
        play(*chains, gradients(*back))

    def step(pair, carry):
        at = pair * (2 * CHUNK)
        both(at, even, at + CHUNK, odd)
        both(at + CHUNK, odd, at + 2 * CHUNK, even)
        return carry

    lax.fori_loop(0, TILE // (2 * CHUNK) - 1, step, 0)
    both(TILE - 2 * CHUNK, even, TILE - CHUNK, odd)
    both(TILE - CHUNK, odd, 0, None)
    zero = jnp.zeros((CH, TILE), F32)
    dm[0] = zero
    dm[TILE + 1] = zero
    for n, (_, row, col, _) in enumerate(peers):
        tile = row * 16 + col
        going[n] = jnp.concatenate(
            [other_cot[rows_to[s, tile]] for s in range(SLOTS)], axis=0
        ).astype(BF16)
    def pack(at, values):
        grads[at:at + values.shape[0]] = values.astype(BF16)

    for side in range(2):
        columns = slice(side * TILE, (side + 1) * TILE)
        pack(side * HID, g_mid[:HID, columns])
        own, other, extra = g_first[0:8, columns], g_first[8:16, columns], g_first[16:32, columns]
        pack(512 + side * 16, jnp.concatenate([jnp.where(flip, other, own), jnp.where(flip, own, other)], axis=0))
        pack(544 + side * 16, extra)
        pack(576 + side * 16, g_mid[HID:HID + 16, columns])
        pack(608 + side * 16, g_out[:, columns])
    pack(640, jnp.concatenate([g_bias[...], jnp.zeros((CH, TILE), F32)], axis=0))
    pack(656, jnp.zeros((16 * PIECE - 656, TILE), F32))


def return_body(going, dm_in, base, grads, weights, source_in, count_in, rate_in,
                adjoint, whole,
                source, count, rate, dm, kernels, back_in, cols_out, cols_in, rows_in, spread, anchor, first_in, mid_sum, second_in, total,
                load_sem, send_sem, recv_sem, hsend_sem, hrecv_sem, s1, r1, s2, r2, s3, r3, in_sem):
    c, i, j = here()
    tables = [
        pltpu.make_async_copy(given, held, in_sem.at[k])
        for k, (given, held) in enumerate(((source_in, source), (count_in, count), (rate_in, rate)))
    ]
    for load in tables:
        load.start()
    lane = lanes()
    barrier = pltpu.get_barrier_semaphore()
    me = c * 4 + i
    across = [(j + d) % 16 for d in range(1, 16)]
    along = [((me + d) % 8 // 4, (me + d) % 4) for d in range(1, 8)]
    for col in across:
        signal_to(barrier, (c, i, col))
    for other in along:
        signal_to(barrier, (*other, j))
    expected = greet(barrier, c, i, j) + 22
    peers = [entry(n, i, j) for n in range(ENTRIES)]
    loads = []
    for n, (_, row, col, _) in enumerate(peers):
        load = pltpu.make_async_copy(weights.at[row * 16 + col], kernels.at[n], load_sem.at[n])
        load.start()
        loads.append(load)
    pl.semaphore_wait(barrier, expected)
    halo = (c, i, j, dm, cols_out, cols_in, rows_in, hsend_sem, hrecv_sem)
    phase1 = [
        remote(grads.at[col], first_in.at[d], s1.at[d], r1.at[d], (c, i, col)) for d, col in enumerate(across)
    ]
    for copy in phase1:
        copy.start()
    sends = []
    for n, (valid, row, col, place) in enumerate(peers):
        copy = remote(going.at[n], back_in.at[place], send_sem.at[n], recv_sem.at[place], (1 - c, row, col))
        sends.append(copy)
        if n < 15:
            copy.start()
        else:
            pl.when(valid == 1)(copy.start)
    dm[...] = dm_in[...]
    edge_columns(dm, cols_out)
    start_halo(halo_copies(*halo))

    for load in tables:
        load.wait()
    for n, (_, row, col, _) in enumerate(peers):
        tile = row * 16 + col
        live = count[0, tile]
        used = peers[n][0]
        for s in range(SLOTS):
            at = source[s, tile]
            keep = (live > s).astype(F32) * used.astype(F32)
            anchor[pl.ds(n * SLOTS + s, 1), :] = (lane[:1] == at).astype(F32) * keep
    anchor[80:, :] = jnp.zeros((TILE - 80, TILE), F32)
    turned = anchor[...].T[:, :80].astype(BF16)
    both = jnp.concatenate([turned, turned], axis=1)

    for copy in phase1:
        copy.wait_recv()
    partial = grads[j].astype(F32)
    for d in range(15):
        partial = partial + first_in[d].astype(F32)
    mid_sum[...] = partial.astype(BF16)
    second_in[me] = partial.astype(BF16)
    phase2 = [
        remote(mid_sum, second_in.at[me], s2.at[d], r2.at[d], (*other, j)) for d, other in enumerate(along)
    ]
    for copy in phase2:
        copy.start()

    wait_halo(*halo)
    sub = lax.broadcasted_iota(jnp.int32, (CH, TILE), 0)
    rates = jnp.zeros((CH, TILE), F32)
    for k in range(CH):
        rates = jnp.where(sub == k, rate[c, k], rates)

    def step(group, carry):
        for k in range(8):
            row = group * 8 + k
            adjoint[pl.ds(row, CH, stride=TILE), :] = base[row] + rates * laplace_row(dm, cols_in, row, lane)
        return carry

    lax.fori_loop(0, TILE // 8, step, 0)

    for d in range(7):
        remote(mid_sum, second_in.at[(me + 7 - d) % 8], s2.at[d], r2.at[d], (*along[d], j)).wait_recv()
    partial = second_in[0].astype(F32)
    for d in range(1, 8):
        partial = partial + second_in[d].astype(F32)
    total[...] = partial.astype(BF16)
    whole[j] = partial.astype(BF16)
    phase3 = [
        remote(total, whole.at[j], s3.at[d], r3.at[d], (c, i, col)) for d, col in enumerate(across)
    ]
    for copy in phase3:
        copy.start()

    for n, (valid, row, col, _) in enumerate(peers):
        arrival = remote(going.at[n], back_in.at[n], send_sem.at[n], recv_sem.at[n], (1 - c, row, col))
        if n < 15:
            arrival.wait_recv()
        else:
            pl.when(valid == 1)(arrival.wait_recv)

            @pl.when(valid == 0)
            def _(n=n):
                back_in[n] = jnp.zeros((SLOTS * CH, TILE), BF16)

    for n in range(ENTRIES):
        loads[n].wait()
    for n in range(ENTRIES):
        made = lax.dot_general(
            back_in[n], kernels[n].reshape(SLOTS * TILE, TILE), NT, preferred_element_type=F32
        )
        for s in range(SLOTS):
            spread[pl.ds(n * SLOTS + s, CH, stride=80), :] = made[s * CH:(s + 1) * CH, s * TILE:(s + 1) * TILE]
    for ch in range(CH):
        cells = spread[ch * 80:(ch + 1) * 80, :]
        high = cells.astype(BF16)
        low = (cells - high.astype(F32)).astype(BF16)
        adjoint[ch * TILE:(ch + 1) * TILE, :] += jnp.dot(
            both, jnp.concatenate([high, low], axis=0), preferred_element_type=F32
        )

    for d in range(15):
        remote(total, whole.at[(j + 15 - d) % 16], s3.at[d], r3.at[d], (c, i, across[d])).wait_recv()
    for n, (valid, _, _, _) in enumerate(peers):
        if n < 15:
            sends[n].wait_send()
        else:
            pl.when(valid == 1)(sends[n].wait_send)
    wait_halo_sent(*halo)
    for copy in phase1 + phase2 + phase3:
        copy.wait_send()


def finish_body(adjoint_in, state_in, whole, adjoint, new_state, o_w_in, o_b_in, o_w_mid, o_b_mid, o_w_out, o_b_out, sem):
    copies = [
        pltpu.make_async_copy(adjoint_in, adjoint, sem.at[0]), pltpu.make_async_copy(state_in, new_state, sem.at[1])
    ]
    for copy in copies:
        copy.start()
    flat = whole[...].astype(F32) * (1.0 / 1048576.0)
    for side in range(2):
        columns = slice(side * TILE, (side + 1) * TILE)
        o_w_mid[:, columns] = flat[side * HID:(side + 1) * HID]
        o_w_in[:, columns] = flat[512 + side * 16:528 + side * 16]
        o_b_in[:, columns] = flat[544 + side * 16:545 + side * 16]
        o_b_mid[:, columns] = flat[576 + side * 16:577 + side * 16]
        o_w_out[:, columns] = flat[608 + side * 16:612 + side * 16]
    sums = jnp.broadcast_to(jnp.sum(flat[640:648], axis=1, keepdims=True), (CH, TILE))
    sub = lax.broadcasted_iota(jnp.int32, (CH, TILE), 0)
    picked = jnp.sum(jnp.where(sub == lanes(), sums, 0.0), axis=0, keepdims=True)
    o_b_out[...] = picked[:, :4]
    for copy in copies:
        copy.wait()


VM = pl.BlockSpec(memory_space=pltpu.VMEM)
SM = pl.BlockSpec(memory_space=pltpu.SMEM)
HB = pl.BlockSpec(memory_space=pltpu.HBM)
DMA = pltpu.SemaphoreType.DMA


def arr(shape, dtype=F32):
    return jax.ShapeDtypeStruct(shape, dtype)


def network_call(*args):
    return pl.pallas_call(
        network_body,
        out_shape=(
            arr((CH * TILE, TILE)),
            arr((TILE + 2, CH, TILE)),
            arr((TILE, CH, TILE)),
            arr((ENTRIES, SLOTS * CH, TILE), BF16),
            arr((16 * PIECE, TILE), BF16),
        ),
        in_specs=[VM] * 5 + [SM] * 4 + [VM] * 5,
        out_specs=(VM,) * 5,
        scratch_shapes=[
            pltpu.VMEM((TILE, CH, TILE), F32),
            pltpu.VMEM((TILE, CH, TILE), F32),
            pltpu.VMEM((HID, TILE), BF16),
            pltpu.VMEM((16, HID), BF16),
            pltpu.VMEM((HID, HID), BF16),
            pltpu.VMEM((HID, HID), BF16),
            pltpu.VMEM((HID, 16), BF16),
            pltpu.VMEM((16, HID), BF16),
            pltpu.VMEM((HID, 4 * TILE), F32),
            pltpu.VMEM((HID, TILE), F32),
            pltpu.VMEM((32, HID), F32),
            pltpu.VMEM((HID + 16, HID), F32),
            pltpu.VMEM((16, HID), F32),
            pltpu.VMEM((CH, TILE), F32),
        ]
        + [
            pltpu.VMEM((32, CHUNK * TILE), BF16),
            pltpu.VMEM((HID + 16, CHUNK * TILE), BF16),
            pltpu.VMEM((HID, CHUNK * TILE), F32),
            pltpu.VMEM((HID, CHUNK * TILE), F32),
            pltpu.VMEM((HID, CHUNK * TILE), BF16),
            pltpu.VMEM((16, CHUNK * TILE), F32),
            pltpu.VMEM((HID, CHUNK * TILE), BF16),
            pltpu.VMEM((HID, CHUNK * TILE), BF16),
            pltpu.VMEM((16, CHUNK * TILE), BF16),
        ] * 2,
        compiler_params=pltpu.CompilerParams(vmem_limit_bytes=48 << 20),
        name="network",
    )(*args)


def shards(state, target, land_mask, diffusivity, coupling, w_in, b_in, w_mid, b_mid, w_out, b_out,
           remap_weight, remap_source, remap_target, remap_count):
    weights = remap_weight.reshape(64, SLOTS, TILE, TILE)
    source = remap_source.reshape(64, SLOTS).T
    rows_to = remap_target.reshape(64, SLOTS).T
    count = remap_count.reshape(1, 64)
    cells = state.reshape(CH * TILE, TILE)
    goal = target.reshape(CH * TILE, TILE)
    land = land_mask.reshape(TILE, TILE)
    ext, cols_in, landed = pl.pallas_call(
        send_body,
        out_shape=(arr((TILE + 2, CH, TILE)), arr((2, CH, TILE)), arr((ENTRIES, SLOTS * CH, TILE), BF16)),
        in_specs=[HB] * 4,
        out_specs=(VM, VM, VM),
        scratch_shapes=[
            pltpu.VMEM((CH * TILE, TILE), F32),
            pltpu.SMEM((SLOTS, 64), jnp.int32),
            pltpu.SMEM((1, 64), jnp.int32),
            pltpu.VMEM((ENTRIES, SLOTS, TILE, TILE), BF16),
            pltpu.VMEM((ENTRIES, SLOTS * CH, TILE), BF16),
            pltpu.VMEM((2, CH, TILE), F32),
            pltpu.VMEM((3, CH, TILE), F32),
            DMA((ENTRIES,)), DMA((ENTRIES,)), DMA((ENTRIES,)), DMA((5,)), DMA((5,)), DMA((3,)),
        ],
        compiler_params=pltpu.CompilerParams(
            collective_id=0, has_side_effects=True, vmem_limit_bytes=24 << 20
        ),
        name="remap_send",
    )(*(pltpu.with_memory_space_constraint(a, pltpu.HBM) for a in (cells, weights, source, count)))

    new_state, dm, base, going, grads = network_call(
        ext, cols_in, landed, goal, land, rows_to, diffusivity, coupling.transpose(0, 2, 1),
        b_out.reshape(1, 4), w_in, b_in.reshape(1, HID), w_mid, b_mid.reshape(1, HID), w_out.T,
    )

    adjoint, whole = pl.pallas_call(
        return_body,
        out_shape=(arr((CH * TILE, TILE)), arr((16, PIECE, TILE), BF16)),
        in_specs=[VM] * 4 + [HB] * 4,
        out_specs=(VM, VM),
        scratch_shapes=[
            pltpu.SMEM((SLOTS, 64), jnp.int32),
            pltpu.SMEM((1, 64), jnp.int32),
            pltpu.SMEM((2, CH), F32),
            pltpu.VMEM((TILE + 2, CH, TILE), F32),
            pltpu.VMEM((ENTRIES, SLOTS, TILE, TILE), BF16),
            pltpu.VMEM((ENTRIES, SLOTS * CH, TILE), BF16),
            pltpu.VMEM((2, CH, TILE), F32),
            pltpu.VMEM((2, CH, TILE), F32),
            pltpu.VMEM((3, CH, TILE), F32),
            pltpu.VMEM((ENTRIES * SLOTS * CH, TILE), F32),
            pltpu.VMEM((TILE, TILE), F32),
            pltpu.VMEM((15, PIECE, TILE), BF16),
            pltpu.VMEM((PIECE, TILE), BF16),
            pltpu.VMEM((8, PIECE, TILE), BF16),
            pltpu.VMEM((PIECE, TILE), BF16),
            DMA((ENTRIES,)), DMA((ENTRIES,)), DMA((ENTRIES,)), DMA((5,)), DMA((5,)),
            DMA((15,)), DMA((15,)), DMA((7,)), DMA((7,)), DMA((15,)), DMA((15,)), DMA((3,)),
        ],
        compiler_params=pltpu.CompilerParams(
            collective_id=1, has_side_effects=True, vmem_limit_bytes=32 << 20
        ),
        name="remap_return",
    )(
        going, dm, base, grads.reshape(16, PIECE, TILE), *(pltpu.with_memory_space_constraint(a, pltpu.HBM) for a in (weights, source, count, diffusivity))
    )
    adjoint, new_state, g_w_in, g_b_in, g_w_mid, g_b_mid, g_w_out, g_b_out = pl.pallas_call(
        finish_body,
        out_shape=(
            arr((CH * TILE, TILE)), arr((CH * TILE, TILE)), arr((16, HID)), arr((1, HID)), arr((HID, HID)), arr((1, HID)),
            arr((4, HID)), arr((1, 4)),
        ),
        in_specs=[VM, VM, VM],
        out_specs=(HB, HB) + (VM,) * 6,
        scratch_shapes=[DMA((2,))],
        compiler_params=pltpu.CompilerParams(vmem_limit_bytes=8 << 20),
        name="finish",
    )(adjoint, new_state, whole.reshape(16 * PIECE, TILE))
    return (
        new_state.reshape(1, CH, TILE, TILE),
        adjoint.reshape(1, CH, TILE, TILE),
        g_w_in,
        g_b_in.reshape(HID),
        g_w_mid,
        g_b_mid.reshape(HID),
        g_w_out.T,
        g_b_out.reshape(4),
    )


def solution(mesh):
    tiles = P("comp", None, "gy", "gx")
    pairs = P("comp", "gy", "gx")
    return jax.shard_map(
        shards,
        mesh=mesh,
        in_specs=(tiles, tiles, pairs) + (P(),) * 8 + (pairs,) * 4,
        out_specs=(tiles, tiles) + (P(),) * 6,
        check_vma=False,
    )
```
